128 devices in a mesh: freq: 32 (over z, x, core), pair: 4 (over y).
Axes of the slice: x: 4, y: 4, z: 4, core: 2. Of those that a mesh axis runs over, the one named last changes fastest.
Arguments:
- voltages: int32 [2048, 103, 2048], P(('pair', 'freq')), may hold values from -8 to 7
- gains: float32 [2048, 96], P(('pair', 'freq')), may hold values from 0.3 to 3
Outputs:
- visibilities: bfloat16 [96, 2, 2048, 2048], P('freq', None, 'pair')
The draws below stay inside these ranges and needn't reach their ends.
All inputs are finite; a program needn't handle non-finite values.
Results may differ from the reference program's by a relative error of at most 0.0078.
Values may be sent and summed in bfloat16 or wider, within the bound.
A program may use at most 128 MiB of HBM per device.

```python
import math
import jax
import jax.numpy as jnp
from jax import lax

INPUTS = 2048
NFFT = 2048
TAPS = 8
SAMPLES = 96
CHANNELS = 96
FRAMES = 103
FIRST = 256


def place_ends(array, stream_key, low, largest):
    shape = array.shape
    index_at = [jax.random.randint(jax.random.fold_in(stream_key, axis), (), 0, shape[axis]) for axis in range(len(shape))]
    array = array.at[tuple(index_at)].set(low)
    longest = shape.index(max(shape))
    index_at[longest] = (index_at[longest] + 1) % shape[longest]
    return array.at[tuple(index_at)].set(largest)


def levels(key, dims, shards, smallest, high):
    def one(position, shards_of):
        draws = jax.random.uniform(jax.random.fold_in(jax.random.fold_in(key, 6), position), (shards_of,), jnp.float32, smallest / len(shards), high / len(shards))
        return jnp.repeat(jnp.exp(draws), dims[position] // shards_of).reshape((-1,) + (1,) * (len(dims) - position - 1))

    loudness = one(*shards[0])
    for cut in shards[1:]:
        loudness = loudness * one(*cut)
    return loudness


def setup_inputs(seed: int = 0) -> dict:
    arg_keys = jax.random.split(jax.random.key(seed), 3)
    return {
        "voltages": place_ends(jax.random.randint(arg_keys[0], (INPUTS, FRAMES, NFFT), -8, 8), jax.random.fold_in(arg_keys[0], 1), -8, 7).astype(jnp.int32),
        "gains": jnp.clip(jnp.exp(math.log(3.0) - 2.3025851 * jax.random.uniform(arg_keys[1], (INPUTS, CHANNELS), jnp.float32) ** levels(arg_keys[1], (INPUTS, CHANNELS), ((0, 128),), -0.2, 0.2)), 0.3, 3.0),
    }


def filter_table():
    positions = jnp.arange(TAPS * NFFT, dtype=jnp.float32)
    span_width = float(TAPS * NFFT)
    window = 0.5 - 0.5 * jnp.cos(2.0 * jnp.pi * (positions + 0.5) / span_width)
    taps_table = window * jnp.sinc((positions - span_width / 2 + 0.5) / NFFT)
    return taps_table.reshape(TAPS, NFFT)

def dft_table(first_bin, count):
    samples = jnp.arange(NFFT, dtype=jnp.int32)
    bin_index = first_bin + jnp.arange(count, dtype=jnp.int32)
    phases = bin_index[:, None] * samples[None, :] % NFFT
    angles = phases.astype(jnp.float32) * (2.0 * math.pi / NFFT)
    amplitude = 0.25 / math.sqrt(NFFT)
    cos_rows = (jnp.cos(angles) * amplitude).astype(jnp.bfloat16)
    sin_rows = (-jnp.sin(angles) * amplitude).astype(jnp.bfloat16)
    return (cos_rows, sin_rows)

def reference(voltages, gains):
    taps_table = filter_table()
    cos_rows, sin_rows = dft_table(FIRST, CHANNELS)
    dft_rows = jnp.concatenate([cos_rows, sin_rows], 0).astype(jnp.float32)
    block_size = 64

    def channelize(parts):
        voltage_block, gain_block = parts
        as_float = voltage_block.astype(jnp.float32)
        filtered = taps_table[0] * as_float[:, 0:SAMPLES, :]
        for tap_index in range(1, TAPS):
            filtered = filtered + taps_table[tap_index] * as_float[:, tap_index:tap_index + SAMPLES, :]
        rounded = lax.optimization_barrier(filtered.astype(jnp.bfloat16))
        filtered = rounded.astype(jnp.float32)
        spectra = jnp.einsum('isn,kn->kis', filtered, dft_rows, precision=lax.Precision.HIGHEST)
        gain_rows = jnp.concatenate([gain_block.T, gain_block.T], 0)
        return (spectra * gain_rows[:, :, None]).astype(jnp.bfloat16)
    voltage_blocks = voltages.reshape(INPUTS // block_size, block_size, FRAMES, NFFT)
    gain_blocks = gains.reshape(INPUTS // block_size, block_size, CHANNELS)
    spectra = lax.map(channelize, (voltage_blocks, gain_blocks))
    spectra = spectra.transpose(1, 0, 2, 3).reshape(2, CHANNELS, INPUTS, SAMPLES)

    def correlate(parts):
        real_part = parts[0].astype(jnp.float32)
        imag_part = parts[1].astype(jnp.float32)

        def outer_product(left_side, right_side):
            return jnp.dot(left_side, right_side.T, precision=lax.Precision.HIGHEST)
        real_sum = outer_product(real_part, real_part) + outer_product(imag_part, imag_part)
        imag_sum = outer_product(imag_part, real_part) - outer_product(real_part, imag_part)
        return (jnp.stack([real_sum, imag_sum]) * (1.0 / SAMPLES)).astype(jnp.bfloat16)
    return lax.map(correlate, (spectra[0], spectra[1]))
```

```python
import functools
import math

import jax
import jax.numpy as jnp
import numpy as np
from jax import lax
from jax.experimental import pallas as pl
from jax.experimental.pallas import tpu as pltpu
from jax.sharding import PartitionSpec as P

NFFT = 2048
TAPS = 8
SAMPLES = 96
FRAMES = 103
FIRST = 256
CHANNELS = 96
CHUNKS = 3
SPECTRA = SAMPLES // CHUNKS
INPUTS = 16
LANES = 128
GROUPS = ((0, 0), (0, 1), (1, 0), (1, 1), (2, 0), (2, 1), (2, 0), (2, 1))
SENT = ((0, 1), (1, 2), (3, 2))
VMEM_LIMIT = 56 * 1024 * 1024


def filter_table():
    positions = np.arange(TAPS * NFFT, dtype=np.float64)
    span_width = float(TAPS * NFFT)
    window = 0.5 - 0.5 * np.cos(2.0 * np.pi * (positions + 0.5) / span_width)
    taps_table = window * np.sinc((positions - span_width / 2 + 0.5) / NFFT)
    return taps_table.astype(np.float32).reshape(TAPS, NFFT)


def dft_table():
    samples = np.arange(NFFT)
    bins = FIRST + np.arange(CHANNELS)
    angles = (bins[:, None] * samples[None, :] % NFFT) * (2.0 * math.pi / NFFT)
    amplitude = 0.25 / math.sqrt(NFFT)
    tables = np.stack([np.cos(angles) * amplitude, -np.sin(angles) * amplitude])
    columns = [tables[part, channel::3] for channel, part in GROUPS]
    return np.concatenate(columns, 0).T.astype(np.float32)


def exchange_lanes(rows):
    lane = lax.broadcasted_iota(jnp.int32, rows[0].shape, 1)
    step = len(rows) // 2
    while step:
        odd = (lane & step) != 0
        out = list(rows)
        for s in range(len(rows)):
            if not s & step:
                low, high = rows[s], rows[s + step]
                out[s] = jnp.where(odd, pltpu.roll(high, step, 1), low)
                out[s + step] = jnp.where(odd, high, pltpu.roll(low, LANES - step, 1))
        rows, step = out, step // 2
    return rows


def spectra_kernel(
    n_freq, n_pair, v_hbm, taps_hbm, dft_hbm, gains_ref, g_ref, h_ref,
    v_buf, taps_raw, taps_buf, dft_buf, gain_buf, f0, f1, y_ref, c2_ref, w_ref,
    v_sem, table_sem, turn_send, turn_recv, own_sem, side_send, side_recv, pass_send, pass_recv,
):
    me = lax.axis_index("freq")
    row = lax.axis_index("pair")
    right, left = lax.rem(row + 1, n_pair), lax.rem(row + n_pair - 1, n_pair)

    tables = [
        pltpu.make_async_copy(taps_hbm, taps_raw, table_sem.at[0]),
        pltpu.make_async_copy(dft_hbm, dft_buf, table_sem.at[1]),
    ]
    tables[0].start()
    history = TAPS - 1
    loads = []
    for chunk in range(CHUNKS):
        first = 0 if chunk == 0 else chunk * SPECTRA + history
        frames = pl.ds(first, (chunk + 1) * SPECTRA + history - first)
        loads.append(pltpu.make_async_copy(v_hbm.at[frames], v_buf.at[frames], v_sem.at[chunk]))
        loads[-1].start()
        if chunk == 0:
            tables[1].start()

    barrier = pltpu.get_barrier_semaphore()

    def greet(j, carry):
        pl.semaphore_signal(barrier, inc=1, device_id={"freq": lax.rem(me + j, n_freq)})
        return carry

    lax.fori_loop(1, n_freq, greet, 0)
    for side in (left, right):
        pl.semaphore_signal(barrier, inc=1, device_id={"pair": side})

    lane = lax.broadcasted_iota(jnp.int32, (CHANNELS, 2 * LANES), 1)
    chan = lax.broadcasted_iota(jnp.int32, (CHANNELS, 2 * LANES), 0)
    wanted = 3 * (lane % 32) + jnp.minimum(lane // 64, 2)
    picks = jnp.where(chan == wanted, 1.0, 0.0).astype(jnp.float32)
    gain_buf[...] = jnp.dot(
        gains_ref[...], picks, precision=lax.Precision.HIGHEST, preferred_element_type=jnp.float32
    )
    tables[0].wait()
    for t in range(TAPS):
        for n in range(NFFT // LANES):
            taps_buf[t, n] = jnp.broadcast_to(
                taps_raw[t : t + 1, n * LANES : (n + 1) * LANES], (8, LANES)
            )

    def filter_slice(chunk, q, out):
        for u in range(2):
            n = 2 * q + u
            col = pl.ds(pl.multiple_of(n * LANES, LANES), LANES)
            taps = [taps_buf[t, n] for t in range(TAPS)]

            def frame(s, half):
                return v_buf[chunk * SPECTRA + s, half * 8 : half * 8 + 8, col].astype(jnp.float32)

            window = [[frame(s, half) for s in range(TAPS)] for half in range(2)]
            for s in range(SPECTRA):
                halves = []
                for half in range(2):
                    if s > 0:
                        window[half] = window[half][1:] + [frame(s + TAPS - 1, half)]
                    terms = [taps[t] * window[half][t] for t in range(TAPS)]
                    while len(terms) > 1:
                        terms = [a + b for a, b in zip(terms[::2], terms[1::2])]
                    halves.append(terms[0])
                out[s * INPUTS : (s + 1) * INPUTS, u * LANES : (u + 1) * LANES] = jnp.concatenate(
                    halves, 0
                ).astype(jnp.bfloat16)

    def transform_slice(q, filtered, start=False):
        rows = pl.ds(pl.multiple_of(q * 2 * LANES, 2 * LANES), 2 * LANES)
        part = jnp.dot(filtered[...], dft_buf[rows, :], preferred_element_type=jnp.float32)
        if start:
            y_ref[...] = part
        else:
            y_ref[...] += part

    def channelize(chunk):
        loads[chunk].wait()
        filter_slice(chunk, 0, f0)
        if chunk == 0:
            tables[1].wait()
        transform_slice(0, f0, True)
        filter_slice(chunk, 1, f1)

        def step(j, carry):
            transform_slice(2 * j - 1, f1)
            filter_slice(chunk, 2 * j, f0)
            transform_slice(2 * j, f0)
            filter_slice(chunk, 2 * j + 1, f1)
            return carry

        lax.fori_loop(1, NFFT // LANES // 4, step, 0)
        transform_slice(NFFT // LANES // 2 - 1, f1)

    def rearrange(chunk):
        def spread(rows, tile):
            for f, block in enumerate(exchange_lanes(rows)):
                w_ref[f, tile] = block

        tile = SENT[chunk][0]
        at = [slice(s * INPUTS, (s + 1) * INPUTS) for s in range(SPECTRA)]
        spread([(y_ref[r, :LANES] * gain_buf[:, :LANES]).astype(jnp.bfloat16) for r in at], tile)
        if chunk == 0:
            c2_ref[...] = y_ref[:, LANES:]
            return
        lane = lax.broadcasted_iota(jnp.int32, (INPUTS, LANES), 1)
        rows = []
        for r in at:
            part = y_ref[r, LANES:]
            if chunk == 1:
                part = jnp.where(lane < 64, c2_ref[r, :], part)
            rows.append((part * gain_buf[:, LANES:]).astype(jnp.bfloat16))
        spread(rows, tile + 1)

    def turn(chunk):
        first, tiles = SENT[chunk]

        def send(j, carry):
            f = lax.rem(me + j, n_freq)
            pltpu.make_async_remote_copy(
                src_ref=w_ref.at[f, pl.ds(first, tiles)],
                dst_ref=g_ref.at[row, pl.ds(first, tiles), me],
                send_sem=turn_send.at[chunk],
                recv_sem=turn_recv.at[chunk],
                device_id={"freq": f},
            ).start()
            return carry

        lax.fori_loop(1, n_freq, send, 0)
        pltpu.make_async_copy(
            w_ref.at[me, pl.ds(first, tiles)], g_ref.at[row, pl.ds(first, tiles), me], own_sem.at[chunk]
        ).start()

    def turn_bytes(chunk):
        first, tiles = SENT[chunk]
        block = w_ref.at[pl.ds(0, n_freq - 1), pl.ds(first, tiles)]
        return pltpu.make_async_remote_copy(
            src_ref=block, dst_ref=block, send_sem=turn_send.at[chunk], recv_sem=turn_recv.at[chunk],
            device_id={"freq": me},
        )

    def turned(chunk):
        first, tiles = SENT[chunk]
        turn_bytes(chunk).wait_recv()
        block = w_ref.at[0, pl.ds(first, tiles)]
        pltpu.make_async_copy(block, block, own_sem.at[chunk]).wait()

    def piece(k, block, half):
        if k == 3:
            pairs = n_freq // 2
            return h_ref.at[block] if half is None else h_ref.at[block, pl.ds(half * pairs // 2, pairs // 2)]
        first, tiles = ((0, 1), (1, 2), (3, 1))[k]
        if half is None:
            return g_ref.at[block, pl.ds(first, tiles)]
        return g_ref.at[block, pl.ds(first, tiles), pl.ds(half * n_freq // 2, n_freq // 2)]

    def side_copy(k, to_right):
        ref = piece(k, row, None)
        return pltpu.make_async_remote_copy(
            src_ref=ref, dst_ref=ref, send_sem=side_send.at[k, int(to_right)], recv_sem=side_recv.at[k, int(to_right)],
            device_id={"pair": right if to_right else left},
        )

    def pass_copy(k, to_right):
        ref = piece(k, left if to_right else right, 0 if to_right else 1)
        return pltpu.make_async_remote_copy(
            src_ref=ref, dst_ref=ref, send_sem=pass_send.at[k, int(to_right)], recv_sem=pass_recv.at[k, int(to_right)],
            device_id={"pair": right if to_right else left},
        )

    def spread(k):
        for to_right in (True, False):
            side_copy(k, to_right).start()

    def forward(k):
        for to_right in (True, False):
            side_copy(k, to_right).wait_recv()
            pass_copy(k, to_right).start()

    channelize(0)
    rearrange(0)
    pl.semaphore_wait(barrier, n_freq + 1)
    turn(0)
    channelize(1)
    turned(0)
    spread(0)
    rearrange(1)
    turn(1)
    channelize(2)
    turned(1)
    spread(1)
    forward(0)
    rearrange(2)
    turn(2)
    turned(2)
    spread(2)
    lane = lax.broadcasted_iota(jnp.int32, (INPUTS, LANES), 1)
    for pair in range(n_freq // 2):
        h_ref[row, pair] = jnp.where(lane < 64, g_ref[row, 4, 2 * pair], g_ref[row, 4, 2 * pair + 1])
    spread(3)
    forward(1)
    forward(2)
    forward(3)
    for k in range(4):
        for to_right in (True, False):
            pass_copy(k, to_right).wait_recv()
    for k in range(4):
        for to_right in (True, False):
            side_copy(k, to_right).wait_send()
            pass_copy(k, to_right).wait_send()
    for chunk in range(CHUNKS):
        turn_bytes(chunk).wait_send()


def spectra_call(n_freq, n_pair, voltages, taps_table, dft, gains):
    bf16 = jnp.bfloat16
    anywhere = pl.BlockSpec(memory_space=pl.ANY)
    vmem = pl.BlockSpec(memory_space=pltpu.VMEM)
    dma = pltpu.SemaphoreType.DMA
    return pl.pallas_call(
        functools.partial(spectra_kernel, n_freq, n_pair),
        out_shape=(
            jax.ShapeDtypeStruct((n_pair, 5, n_freq, INPUTS, LANES), bf16),
            jax.ShapeDtypeStruct((n_pair, n_freq // 2, INPUTS, LANES), bf16),
        ),
        in_specs=[anywhere, anywhere, anywhere, vmem],
        out_specs=(vmem, vmem),
        scratch_shapes=[
            pltpu.VMEM((FRAMES, INPUTS, NFFT), jnp.int32),
            pltpu.VMEM((TAPS, NFFT), jnp.float32),
            pltpu.VMEM((TAPS, NFFT // LANES, 8, LANES), jnp.float32),
            pltpu.VMEM((NFFT, 2 * LANES), bf16),
            pltpu.VMEM((INPUTS, 2 * LANES), jnp.float32),
            pltpu.VMEM((SPECTRA * INPUTS, 2 * LANES), bf16),
            pltpu.VMEM((SPECTRA * INPUTS, 2 * LANES), bf16),
            pltpu.VMEM((SPECTRA * INPUTS, 2 * LANES), jnp.float32),
            pltpu.VMEM((SPECTRA * INPUTS, LANES), jnp.float32),
            pltpu.VMEM((n_freq, 5, INPUTS, LANES), bf16),
            dma((CHUNKS,)), dma((2,)), dma((CHUNKS,)), dma((CHUNKS,)), dma((CHUNKS,)),
            dma((4, 2)), dma((4, 2)), dma((4, 2)), dma((4, 2)),
        ],
        compiler_params=pltpu.CompilerParams(
            collective_id=0, has_side_effects=True, vmem_limit_bytes=VMEM_LIMIT
        ),
    )(voltages, taps_table, dft, gains)


def correlate_kernel(n_freq, n_pair, cols, g_ref, h_ref, out_ref, x_ref, l_ref):
    channel, block = pl.program_id(0), pl.program_id(1)
    row = lax.axis_index("pair")
    lane = lax.broadcasted_iota(jnp.int32, (INPUTS, LANES), 1)
    low = lane < 64
    real_slot = (lane & 32) == 0
    zero = jnp.zeros((INPUTS, LANES), jnp.bfloat16)

    @pl.when((channel == 0) & (block == 0))
    def _():
        def gather(p, carry):
            for src in range(n_freq):
                t0, t1, t2, t3 = (g_ref[p, t, src] for t in range(4))
                t4 = h_ref[p, src // 2]
                if src % 2:
                    t4 = pltpu.roll(t4, 64, 1)
                at = pl.ds(pl.multiple_of((p * n_freq + src) * INPUTS, INPUTS), INPUTS)
                x_ref[0, at, :LANES] = jnp.where(low, t0, pltpu.roll(t1, 64, 1))
                x_ref[1, at, :LANES] = jnp.where(low, pltpu.roll(t0, 64, 1), t1)
                x_ref[2, at, :LANES] = t2
                x_ref[0, at, LANES:] = t3
                x_ref[1, at, LANES:] = t3
                x_ref[2, at, LANES:] = t4
            return carry

        lax.fori_loop(0, n_pair, gather, 0)

        def rows(src, carry):
            at = pl.ds(pl.multiple_of((row * n_freq + src) * INPUTS, INPUTS), INPUTS)
            for c in range(3):
                for k in range(2):
                    x = x_ref[c, at, k * LANES : (k + 1) * LANES]
                    if k:
                        x = jnp.where(low == (c != 1), x, zero)
                    turned = jnp.where(real_slot, pltpu.roll(x, 96, 1), -pltpu.roll(x, 32, 1))
                    to = pl.multiple_of(src * INPUTS, INPUTS)
                    l_ref[c, pl.ds(to, INPUTS), k * LANES : (k + 1) * LANES] = x
                    l_ref[c, pl.ds(n_freq * INPUTS + to, INPUTS), k * LANES : (k + 1) * LANES] = turned
            return carry

        lax.fori_loop(0, n_freq, rows, 0)

    at = pl.ds(pl.multiple_of(block * cols, cols), cols)
    sums = lax.dot_general(
        l_ref[channel], x_ref[channel, at, :], (((1,), (1,)), ((), ())), preferred_element_type=jnp.float32
    )
    sums = (sums * (1.0 / SAMPLES)).astype(jnp.bfloat16)
    out_ref[0, 0] = sums[: n_freq * INPUTS]
    out_ref[0, 1] = sums[n_freq * INPUTS :]


def correlate_call(n_freq, n_pair, spectra, packed):
    rows, columns, cols = n_freq * INPUTS, n_pair * n_freq * INPUTS, 512
    vmem = pl.BlockSpec(memory_space=pltpu.VMEM)
    return pl.pallas_call(
        functools.partial(correlate_kernel, n_freq, n_pair, cols),
        grid=(3, columns // cols),
        out_shape=jax.ShapeDtypeStruct((3, 2, rows, columns), jnp.bfloat16),
        in_specs=[vmem, vmem],
        out_specs=pl.BlockSpec((1, 2, rows, cols), lambda c, b: (c, 0, 0, b)),
        scratch_shapes=[
            pltpu.VMEM((3, columns, 2 * LANES), jnp.bfloat16),
            pltpu.VMEM((3, 2 * rows, 2 * LANES), jnp.bfloat16),
        ],
        compiler_params=pltpu.CompilerParams(vmem_limit_bytes=VMEM_LIMIT),
    )(spectra, packed)


def solution(mesh):
    n_freq, n_pair = mesh.shape["freq"], mesh.shape["pair"]
    taps_table = jnp.asarray(filter_table())
    dft = jnp.asarray(dft_table()).astype(jnp.bfloat16)

    def body(voltages, gains):
        frames = voltages.transpose(1, 0, 2)
        spectra, packed = spectra_call(n_freq, n_pair, frames, taps_table, dft, gains)
        return correlate_call(n_freq, n_pair, spectra, packed)

    placed = (P(("pair", "freq"), None, None), P(("pair", "freq"), None))
    return jax.shard_map(
        body, mesh=mesh, in_specs=placed, out_specs=P("freq", None, "pair", None), check_vma=False
    )
```

```python
import functools
import math

import jax
import jax.numpy as jnp
import numpy as np
from jax import lax
from jax.experimental import pallas as pl
from jax.experimental.pallas import tpu as pltpu
from jax.sharding import PartitionSpec as P

NFFT = 2048
TAPS = 8
SAMPLES = 96
FRAMES = 103
FIRST = 256
CHANNELS = 96
CHUNKS = 3
SPECTRA = SAMPLES // CHUNKS
INPUTS = 16
LANES = 128
GROUPS = ((0, 0), (0, 1), (1, 0), (1, 1), (2, 0), (2, 1), (2, 0), (2, 1))
SENT = ((0, 1), (1, 2), (3, 2))
VMEM_LIMIT = 36 * 1024 * 1024


def filter_table():
    positions = np.arange(TAPS * NFFT, dtype=np.float64)
    span_width = float(TAPS * NFFT)
    window = 0.5 - 0.5 * np.cos(2.0 * np.pi * (positions + 0.5) / span_width)
    taps_table = window * np.sinc((positions - span_width / 2 + 0.5) / NFFT)
    return taps_table.astype(np.float32).reshape(TAPS, NFFT)


def dft_table():
    samples = np.arange(NFFT)
    bins = FIRST + np.arange(CHANNELS)
    angles = (bins[:, None] * samples[None, :] % NFFT) * (2.0 * math.pi / NFFT)
    amplitude = 0.25 / math.sqrt(NFFT)
    tables = np.stack([np.cos(angles) * amplitude, -np.sin(angles) * amplitude])
    columns = [tables[part, channel::3] for channel, part in GROUPS]
    return np.concatenate(columns, 0).T.astype(np.float32)


def exchange_lanes(rows):
    lane = lax.broadcasted_iota(jnp.int32, rows[0].shape, 1)
    step = len(rows) // 2
    while step:
        odd = (lane & step) != 0
        out = list(rows)
        for s in range(len(rows)):
            if not s & step:
                low, high = rows[s], rows[s + step]
                out[s] = jnp.where(odd, pltpu.roll(high, step, 1), low)
                out[s + step] = jnp.where(odd, high, pltpu.roll(low, LANES - step, 1))
        rows, step = out, step // 2
    return rows


def spectra_kernel(
    n_freq, n_pair, v_hbm, taps_hbm, dft_hbm, gains_ref, x_ref, mid_ref, end_ref, x4_ref, l_ref,
    v_buf, taps_raw, taps_buf, dft_buf, gain_buf, f0, f1, y_ref, c2_ref, w_ref, t0_ref,
    v_sem, table_sem, turn_send, turn_recv, own_sem, side_send, side_recv, pass_send, pass_recv,
):
    me = lax.axis_index("freq")
    row = lax.axis_index("pair")
    right, left = lax.rem(row + 1, n_pair), lax.rem(row + n_pair - 1, n_pair)

    tables = [
        pltpu.make_async_copy(taps_hbm, taps_raw, table_sem.at[0]),
        pltpu.make_async_copy(dft_hbm, dft_buf, table_sem.at[1]),
    ]
    tables[0].start()
    history = TAPS - 1

    def first_load(piece):
        frames = pl.ds(0, SPECTRA + history)
        cols = pl.ds(pl.multiple_of(piece * (NFFT // 4), NFFT // 4), NFFT // 4)
        return pltpu.make_async_copy(
            v_hbm.at[frames, :, cols], v_buf.at[frames, :, cols], v_sem.at[piece]
        )

    def later_load(chunk):
        frames = pl.ds(chunk * SPECTRA + history, SPECTRA)
        return pltpu.make_async_copy(v_hbm.at[frames], v_buf.at[frames], v_sem.at[3 + chunk])

    for piece in range(4):
        first_load(piece).start()
        if piece == 0:
            tables[1].start()

    barrier = pltpu.get_barrier_semaphore()

    def greet(j, carry):
        pl.semaphore_signal(barrier, inc=1, device_id={"freq": lax.rem(me + j, n_freq)})
        return carry

    lax.fori_loop(1, n_freq, greet, 0)
    for side in (left, right):
        pl.semaphore_signal(barrier, inc=1, device_id={"pair": side})

    lane = lax.broadcasted_iota(jnp.int32, (CHANNELS, 2 * LANES), 1)
    chan = lax.broadcasted_iota(jnp.int32, (CHANNELS, 2 * LANES), 0)
    wanted = 3 * (lane % 32) + jnp.minimum(lane // 64, 2)
    picks = jnp.where(chan == wanted, 1.0, 0.0).astype(jnp.float32)
    gain_buf[...] = jnp.dot(
        gains_ref[...], picks, precision=lax.Precision.HIGHEST, preferred_element_type=jnp.float32
    )
    tables[0].wait()
    for t in range(TAPS):
        for n in range(NFFT // LANES):
            taps_buf[t, n] = jnp.broadcast_to(
                taps_raw[t : t + 1, n * LANES : (n + 1) * LANES], (8, LANES)
            )

    def filter_slice(chunk, q, out):
        for u in range(2):
            n = 2 * q + u
            col = pl.ds(pl.multiple_of(n * LANES, LANES), LANES)
            taps = [taps_buf[t, n] for t in range(TAPS)]

            def frame(s, half):
                return v_buf[chunk * SPECTRA + s, half * 8 : half * 8 + 8, col].astype(jnp.float32)

            window = [[frame(s, half) for s in range(TAPS)] for half in range(2)]
            for s in range(SPECTRA):
                halves = []
                for half in range(2):
                    if s > 0:
                        window[half] = window[half][1:] + [frame(s + TAPS - 1, half)]
                    terms = [taps[t] * window[half][t] for t in range(TAPS)]
                    while len(terms) > 1:
                        terms = [a + b for a, b in zip(terms[::2], terms[1::2])]
                    halves.append(terms[0])
                out[s * INPUTS : (s + 1) * INPUTS, u * LANES : (u + 1) * LANES] = jnp.concatenate(
                    halves, 0
                ).astype(jnp.bfloat16)

    def transform_slice(q, filtered, start=False):
        rows = pl.ds(pl.multiple_of(q * 2 * LANES, 2 * LANES), 2 * LANES)
        part = jnp.dot(filtered[...], dft_buf[rows, :], preferred_element_type=jnp.float32)
        if start:
            y_ref[...] = part
        else:
            y_ref[...] += part

    def channelize(chunk, serve=None):
        if chunk == 0:
            first_load(0).wait()
        else:
            later_load(chunk).wait()
        if chunk == 1:
            later_load(2).start()
        filter_slice(chunk, 0, f0)
        if chunk == 0:
            tables[1].wait()
        transform_slice(0, f0, True)
        filter_slice(chunk, 1, f1)

        def step(j, carry):
            if chunk == 0:
                first_load(j).wait()
                pl.when(j == 2)(lambda: later_load(1).start())
            if serve is not None:
                pl.when(j == 3)(serve)
            transform_slice(2 * j - 1, f1)
            filter_slice(chunk, 2 * j, f0)
            transform_slice(2 * j, f0)
            filter_slice(chunk, 2 * j + 1, f1)
            return carry

        lax.fori_loop(1, NFFT // LANES // 4, step, 0)
        transform_slice(NFFT // LANES // 2 - 1, f1)

    def rearrange(chunk):
        def spread(rows, tile):
            for f, block in enumerate(exchange_lanes(rows)):
                w_ref[f, tile] = block

        tile = SENT[chunk][0]
        at = [slice(s * INPUTS, (s + 1) * INPUTS) for s in range(SPECTRA)]
        spread([(y_ref[r, :LANES] * gain_buf[:, :LANES]).astype(jnp.bfloat16) for r in at], tile)
        if chunk == 0:
            c2_ref[...] = y_ref[:, LANES:]
            return
        lane = lax.broadcasted_iota(jnp.int32, (INPUTS, LANES), 1)
        rows = []
        for r in at:
            part = y_ref[r, LANES:]
            if chunk == 1:
                part = jnp.where(lane < 64, c2_ref[r, :], part)
            rows.append((part * gain_buf[:, LANES:]).astype(jnp.bfloat16))
        spread(rows, tile + 1)

    def landing(chunk, block):
        if chunk == 0:
            return t0_ref.at[:, block]
        return (mid_ref if chunk == 1 else end_ref).at[:, block]

    z, x, core = me // 8, lax.rem(me // 2, 4), lax.rem(me, 2)
    steps = [(dz, dx, dc) for dz in (2, 1, 3, 0) for dx in (2, 1, 3, 0) for dc in (0, 1)]
    steps.sort(key=lambda d: -min(d[0], 4 - d[0]) - min(d[1], 4 - d[1]))
    peers = [
        lax.rem(z + dz, 4) * 8 + lax.rem(x + dx, 4) * 2 + lax.rem(core + dc, 2)
        for dz, dx, dc in steps
        if dz or dx or dc
    ]

    def own_copy(chunk):
        first, tiles = SENT[chunk]
        return pltpu.make_async_copy(
            w_ref.at[me, pl.ds(first, tiles)], landing(chunk, row).at[:, me], own_sem.at[chunk]
        )

    def turn(chunk):
        first, tiles = SENT[chunk]
        for f in peers:
            pltpu.make_async_remote_copy(
                src_ref=w_ref.at[f, pl.ds(first, tiles)], dst_ref=landing(chunk, row).at[:, me],
                send_sem=turn_send.at[chunk], recv_sem=turn_recv.at[chunk], device_id={"freq": f},
            ).start()
        own_copy(chunk).start()

    def turn_bytes(chunk):
        first, tiles = SENT[chunk]
        block = w_ref.at[pl.ds(0, n_freq - 1), pl.ds(first, tiles)]
        return pltpu.make_async_remote_copy(
            src_ref=block, dst_ref=block, send_sem=turn_send.at[chunk], recv_sem=turn_recv.at[chunk],
            device_id={"freq": me},
        )

    def turned(chunk):
        turn_bytes(chunk).wait_recv()
        own_copy(chunk).wait()

    def piece(k, block, half):
        if k == 3:
            return x4_ref.at[block, pl.ds(half * n_freq // 4, n_freq // 4)]
        ref = landing(k, block).at[:, pl.ds(half * n_freq // 2, n_freq // 2)]
        return ref.at[0] if k == 2 else ref

    def side_copy(k, way, half):
        ref = piece(k, row, half)
        return pltpu.make_async_remote_copy(
            src_ref=ref, dst_ref=ref, send_sem=side_send.at[k, way, half], recv_sem=side_recv.at[k, way, half],
            device_id={"pair": right if way == 0 else left},
        )

    def pass_copy(k, way):
        ref = piece(k, left if way == 0 else right, way)
        return pltpu.make_async_remote_copy(
            src_ref=ref, dst_ref=ref, send_sem=pass_send.at[k, way], recv_sem=pass_recv.at[k, way],
            device_id={"pair": right if way == 0 else left},
        )

    def spread(*pieces):
        for first in (True, False):
            for k in pieces:
                for way in range(2):
                    side_copy(k, way, way if first else 1 - way).start()

    def forward(*pieces):
        for k in pieces:
            for way in range(2):
                side_copy(k, way, way).wait_recv()
                pass_copy(k, way).start()

    def arrived(*pieces):
        for k in pieces:
            for way in range(2):
                side_copy(k, way, 1 - way).wait_recv()

    def passed(*pieces):
        for k in pieces:
            for way in range(2):
                pass_copy(k, way).wait_recv()

    low = lax.broadcasted_iota(jnp.int32, (INPUTS, LANES), 1) < 64
    real_slot = (lax.broadcasted_iota(jnp.int32, (INPUTS, LANES), 1) & 32) == 0
    zero = jnp.zeros((INPUTS, LANES), jnp.bfloat16)

    def sort(block):
        def one(src, carry):
            t0, t1 = t0_ref[0, block, src], mid_ref[0, block, src]
            x_ref[0, block, src] = jnp.where(low, t0, pltpu.roll(t1, 64, 1))
            x_ref[1, block, src] = jnp.where(low, pltpu.roll(t0, 64, 1), t1)
            return carry

        lax.fori_loop(0, n_freq, one, 0, unroll=4)

    def put_rows(c, k, src, x):
        turned_x = jnp.where(real_slot, pltpu.roll(x, 96, 1), -pltpu.roll(x, 32, 1))
        l_ref[c, 0, src, :, k * LANES : (k + 1) * LANES] = x
        l_ref[c, 1, src, :, k * LANES : (k + 1) * LANES] = turned_x

    def rows_early():
        def one(src, carry):
            for c in range(4):
                put_rows(c, 0, src, x_ref[c, row, src] if c < 2 else mid_ref[1, row, src])
            return carry

        lax.fori_loop(0, n_freq, one, 0)

    def rows_late():
        def one(src, carry):
            t3, t4 = end_ref[0, row, src], end_ref[1, row, src]
            put_rows(0, 1, src, jnp.where(low, t3, zero))
            put_rows(1, 1, src, jnp.where(low, zero, t3))
            put_rows(2, 1, src, jnp.where(low, t4, zero))
            put_rows(3, 1, src, jnp.where(low, zero, t4))
            return carry

        lax.fori_loop(0, n_freq, one, 0)

    def after_first():
        turned(0)
        spread(0)

    def after_second():
        turned(1)
        spread(1)

    channelize(0)
    rearrange(0)
    pl.semaphore_wait(barrier, n_freq + 1)
    turn(0)
    channelize(1, after_first)
    rearrange(1)
    turn(1)
    forward(0)
    channelize(2, after_second)
    rearrange(2)
    turn(2)
    sort(row)
    rows_early()
    forward(1)
    turned(2)
    for src in range(n_freq // 2):
        x4_ref[row, src] = jnp.where(low, end_ref[1, row, src], end_ref[1, row, src + n_freq // 2])
    spread(2, 3)
    rows_late()
    arrived(0, 1)
    sort(right)
    sort(left)
    forward(2, 3)
    passed(0, 1)
    sort(lax.rem(row + 2, n_pair))
    arrived(2, 3)
    for k in range(4):
        for way in range(2):
            for half in range(2):
                side_copy(k, way, half).wait_send()
            pass_copy(k, way).wait_send()
    for chunk in range(CHUNKS):
        turn_bytes(chunk).wait_send()
    passed(2, 3)


def spectra_call(n_freq, n_pair, voltages, taps_table, dft, gains):
    bf16 = jnp.bfloat16
    anywhere = pl.BlockSpec(memory_space=pl.ANY)
    vmem = pl.BlockSpec(memory_space=pltpu.VMEM)
    dma = pltpu.SemaphoreType.DMA
    in_hbm = functools.partial(pltpu.with_memory_space_constraint, memory_space=pltpu.HBM)
    return pl.pallas_call(
        functools.partial(spectra_kernel, n_freq, n_pair),
        out_shape=(
            pltpu.VMEM((2, n_pair, n_freq, INPUTS, LANES), bf16),
            pltpu.VMEM((2, n_pair, n_freq, INPUTS, LANES), bf16),
            pltpu.VMEM((2, n_pair, n_freq, INPUTS, LANES), bf16),
            pltpu.VMEM((n_pair, n_freq // 2, INPUTS, LANES), bf16),
            pltpu.VMEM((4, 2, n_freq, INPUTS, 2 * LANES), bf16),
        ),
        in_specs=[anywhere, anywhere, anywhere, vmem],
        out_specs=(vmem,) * 5,
        scratch_shapes=[
            pltpu.VMEM((FRAMES, INPUTS, NFFT), jnp.int32),
            pltpu.VMEM((TAPS, NFFT), jnp.float32),
            pltpu.VMEM((TAPS, NFFT // LANES, 8, LANES), jnp.float32),
            pltpu.VMEM((NFFT, 2 * LANES), bf16),
            pltpu.VMEM((INPUTS, 2 * LANES), jnp.float32),
            pltpu.VMEM((SPECTRA * INPUTS, 2 * LANES), bf16),
            pltpu.VMEM((SPECTRA * INPUTS, 2 * LANES), bf16),
            pltpu.VMEM((SPECTRA * INPUTS, 2 * LANES), jnp.float32),
            pltpu.VMEM((SPECTRA * INPUTS, LANES), jnp.float32),
            pltpu.VMEM((n_freq, 5, INPUTS, LANES), bf16),
            pltpu.VMEM((1, n_pair, n_freq, INPUTS, LANES), bf16),
            dma((6,)), dma((2,)), dma((CHUNKS,)), dma((CHUNKS,)), dma((CHUNKS,)),
            dma((4, 2, 2)), dma((4, 2, 2)), dma((4, 2)), dma((4, 2)),
        ],
        compiler_params=pltpu.CompilerParams(
            collective_id=0, has_side_effects=True, vmem_limit_bytes=VMEM_LIMIT
        ),
    )(*map(in_hbm, (voltages, taps_table, dft, gains)))


def correlate_kernel(n_freq, n_pair, x_ref, mid_ref, end_ref, x4_ref, l_ref, out_hbm, out_buf, sem):
    rows, half = n_freq * INPUTS, n_freq * INPUTS // 2

    def copy(c, p):
        cols = pl.ds(pl.multiple_of(p * rows, rows), rows)
        return pltpu.make_async_copy(out_buf.at[c, p], out_hbm.at[c, :, :, cols], sem.at[c, p])

    for c in range(3):

        def block(p, carry):
            for h in range(2):
                srcs = slice(h * n_freq // 2, (h + 1) * n_freq // 2)
                first = (x_ref[c, p, srcs] if c < 2 else mid_ref[1, p, srcs]).reshape(half, LANES)
                last = (x4_ref[p] if c == 2 else end_ref[0, p, srcs]).reshape(half, LANES)
                side = l_ref[3 if c == 2 and h else c].reshape(2 * rows, 2 * LANES)
                sums = lax.dot_general(
                    side, jnp.concatenate([first, last], 1), (((1,), (1,)), ((), ())),
                    preferred_element_type=jnp.float32,
                )
                sums = (sums * (1.0 / SAMPLES)).astype(jnp.bfloat16)
                out_buf[c, p, 0, :, h * half : (h + 1) * half] = sums[:rows]
                out_buf[c, p, 1, :, h * half : (h + 1) * half] = sums[rows:]
            copy(c, p).start()
            return carry

        lax.fori_loop(0, n_pair, block, 0, unroll=True)

    for c in range(3):
        for p in range(n_pair):
            copy(c, p).wait()


def correlate_call(n_freq, n_pair, *spectra):
    rows, columns = n_freq * INPUTS, n_pair * n_freq * INPUTS
    vmem = pl.BlockSpec(memory_space=pltpu.VMEM)
    return pl.pallas_call(
        functools.partial(correlate_kernel, n_freq, n_pair),
        out_shape=jax.ShapeDtypeStruct((3, 2, rows, columns), jnp.bfloat16),
        in_specs=[vmem] * 5,
        out_specs=pl.BlockSpec(memory_space=pl.ANY),
        scratch_shapes=[
            pltpu.VMEM((3, n_pair, 2, rows, rows), jnp.bfloat16),
            pltpu.SemaphoreType.DMA((3, n_pair)),
        ],
        compiler_params=pltpu.CompilerParams(vmem_limit_bytes=VMEM_LIMIT),
    )(*(pltpu.with_memory_space_constraint(x, pltpu.VMEM) for x in spectra))


def solution(mesh):
    n_freq, n_pair = mesh.shape["freq"], mesh.shape["pair"]
    taps_table = jnp.asarray(filter_table())
    dft = jnp.asarray(dft_table()).astype(jnp.bfloat16)

    def body(voltages, gains):
        frames = voltages.transpose(1, 0, 2)
        return correlate_call(n_freq, n_pair, *spectra_call(n_freq, n_pair, frames, taps_table, dft, gains))

    placed = (P(("pair", "freq"), None, None), P(("pair", "freq"), None))
    return jax.shard_map(
        body, mesh=mesh, in_specs=placed, out_specs=P("freq", None, "pair", None), check_vma=False
    )
```

```python
import functools
import math

import jax
import jax.numpy as jnp
import numpy as np
from jax import lax
from jax.experimental import pallas as pl
from jax.experimental.pallas import tpu as pltpu
from jax.sharding import PartitionSpec as P

NFFT = 2048
TAPS = 8
SAMPLES = 96
FRAMES = 103
FIRST = 256
CHANNELS = 96
CHUNKS = 3
SPECTRA = SAMPLES // CHUNKS
INPUTS = 16
LANES = 128
GROUPS = ((0, 0), (0, 1), (1, 0), (1, 1), (2, 0), (2, 1), (2, 0), (2, 1))
SENT = ((0, 1), (1, 2), (3, 2))
VMEM_LIMIT = 36 * 1024 * 1024


def filter_table():
    positions = np.arange(TAPS * NFFT, dtype=np.float64)
    span_width = float(TAPS * NFFT)
    window = 0.5 - 0.5 * np.cos(2.0 * np.pi * (positions + 0.5) / span_width)
    taps_table = window * np.sinc((positions - span_width / 2 + 0.5) / NFFT)
    return taps_table.astype(np.float32).reshape(TAPS, NFFT)


def dft_table():
    samples = np.arange(NFFT)
    bins = FIRST + np.arange(CHANNELS)
    angles = (bins[:, None] * samples[None, :] % NFFT) * (2.0 * math.pi / NFFT)
    amplitude = 0.25 / math.sqrt(NFFT)
    tables = np.stack([np.cos(angles) * amplitude, -np.sin(angles) * amplitude])
    columns = [tables[part, channel::3] for channel, part in GROUPS]
    return np.concatenate(columns, 0).T.astype(np.float32)


def exchange_lanes(rows):
    lane = lax.broadcasted_iota(jnp.int32, rows[0].shape, 1)
    step = len(rows) // 2
    while step:
        odd = (lane & step) != 0
        out = list(rows)
        for s in range(len(rows)):
            if not s & step:
                low, high = rows[s], rows[s + step]
                out[s] = jnp.where(odd, pltpu.roll(high, step, 1), low)
                out[s + step] = jnp.where(odd, high, pltpu.roll(low, LANES - step, 1))
        rows, step = out, step // 2
    return rows


def spectra_kernel(
    n_freq, n_pair, v_hbm, taps_hbm, dft_hbm, gains_hbm, x_out, mid_out, end_out, x4_out, l_out,
    v_buf, gains_ref, taps_raw, taps_buf, dft_buf, gain_buf, f0, f1, y_ref, c2_ref, w_ref, t0_ref, x_ref, mid_ref, end_ref, x4_ref, l_ref,
    v_sem, table_sem, turn_send, turn_recv, own_sem, out_sem, side_send, side_recv, pass_send, pass_recv,
):
    me = lax.axis_index("freq")
    row = lax.axis_index("pair")
    right, left = lax.rem(row + 1, n_pair), lax.rem(row + n_pair - 1, n_pair)

    tables = [
        pltpu.make_async_copy(taps_hbm, taps_raw, table_sem.at[0]),
        pltpu.make_async_copy(dft_hbm, dft_buf, table_sem.at[1]),
        pltpu.make_async_copy(gains_hbm, gains_ref, table_sem.at[2]),
    ]
    tables[0].start()
    history = TAPS - 1

    def first_load(piece):
        frames = pl.ds(0, SPECTRA + history)
        cols = pl.ds(pl.multiple_of(piece * (NFFT // 4), NFFT // 4), NFFT // 4)
        return pltpu.make_async_copy(
            v_hbm.at[frames, :, cols], v_buf.at[frames, :, cols], v_sem.at[piece]
        )

    def later_load(chunk):
        frames = pl.ds(chunk * SPECTRA + history, SPECTRA)
        return pltpu.make_async_copy(v_hbm.at[frames], v_buf.at[frames], v_sem.at[3 + chunk])

    first_load(0).start()
    tables[1].start()
    tables[2].start()
    first_load(1).start()

    barrier = pltpu.get_barrier_semaphore()

    def greet(j, carry):
        pl.semaphore_signal(barrier, inc=1, device_id={"freq": lax.rem(me + j, n_freq)})
        return carry

    lax.fori_loop(1, n_freq, greet, 0)
    for side in (left, right):
        pl.semaphore_signal(barrier, inc=1, device_id={"pair": side})

    tables[0].wait()
    for t in range(TAPS):
        for n in range(NFFT // LANES):
            taps_buf[t, n] = jnp.broadcast_to(
                taps_raw[t : t + 1, n * LANES : (n + 1) * LANES], (8, LANES)
            )

    def filter_slice(chunk, q, out):
        for u in range(2):
            n = 2 * q + u
            col = pl.ds(pl.multiple_of(n * LANES, LANES), LANES)
            taps = [taps_buf[t, n] for t in range(TAPS)]

            def frame(s, half):
                return v_buf[chunk * SPECTRA + s, half * 8 : half * 8 + 8, col].astype(jnp.float32)

            window = [[frame(s, half) for s in range(TAPS)] for half in range(2)]
            for s in range(SPECTRA):
                halves = []
                for half in range(2):
                    if s > 0:
                        window[half] = window[half][1:] + [frame(s + TAPS - 1, half)]
                    terms = [taps[t] * window[half][t] for t in range(TAPS)]
                    while len(terms) > 1:
                        terms = [a + b for a, b in zip(terms[::2], terms[1::2])]
                    halves.append(terms[0])
                out[s * INPUTS : (s + 1) * INPUTS, u * LANES : (u + 1) * LANES] = jnp.concatenate(
                    halves, 0
                ).astype(jnp.bfloat16)

    def transform_slice(q, filtered, start=False):
        rows = pl.ds(pl.multiple_of(q * 2 * LANES, 2 * LANES), 2 * LANES)
        part = jnp.dot(filtered[...], dft_buf[rows, :], preferred_element_type=jnp.float32)
        if start:
            y_ref[...] = part
        else:
            y_ref[...] += part

    def channelize(chunk, serve=()):
        if chunk == 0:
            first_load(0).wait()
            first_load(2).start()
        else:
            later_load(chunk).wait()
        if chunk == 1:
            later_load(2).start()
        filter_slice(chunk, 0, f0)
        if chunk == 0:
            tables[1].wait()
        transform_slice(0, f0, True)
        filter_slice(chunk, 1, f1)

        def step(j, carry):
            if chunk == 0:
                first_load(j).wait()
                pl.when(j == 1)(lambda: first_load(3).start())
                pl.when(j == 2)(lambda: later_load(1).start())
            for when, who, what in serve:
                pl.when((j == when) & who)(what)
            transform_slice(2 * j - 1, f1)
            filter_slice(chunk, 2 * j, f0)
            transform_slice(2 * j, f0)
            filter_slice(chunk, 2 * j + 1, f1)
            return carry

        lax.fori_loop(1, NFFT // LANES // 4, step, 0)
        transform_slice(NFFT // LANES // 2 - 1, f1)

    def order_gains():
        tables[2].wait()
        lane = lax.broadcasted_iota(jnp.int32, (CHANNELS, 2 * LANES), 1)
        chan = lax.broadcasted_iota(jnp.int32, (CHANNELS, 2 * LANES), 0)
        wanted = 3 * (lane % 32) + jnp.minimum(lane // 64, 2)
        picks = jnp.where(chan == wanted, 1.0, 0.0).astype(jnp.float32)
        gain_buf[...] = jnp.dot(
            gains_ref[...], picks, precision=lax.Precision.HIGHEST, preferred_element_type=jnp.float32
        )

    def rearrange(chunk):
        def spread(rows, tile):
            for f, block in enumerate(exchange_lanes(rows)):
                w_ref[f, tile] = block

        tile = SENT[chunk][0]
        at = [slice(s * INPUTS, (s + 1) * INPUTS) for s in range(SPECTRA)]
        spread([(y_ref[r, :LANES] * gain_buf[:, :LANES]).astype(jnp.bfloat16) for r in at], tile)
        if chunk == 0:
            c2_ref[...] = y_ref[:, LANES:]
            return
        lane = lax.broadcasted_iota(jnp.int32, (INPUTS, LANES), 1)
        rows = []
        for r in at:
            part = y_ref[r, LANES:]
            if chunk == 1:
                part = jnp.where(lane < 64, c2_ref[r, :], part)
            rows.append((part * gain_buf[:, LANES:]).astype(jnp.bfloat16))
        spread(rows, tile + 1)

    def landing(chunk, block):
        if chunk == 2:
            return end_ref
        return (mid_ref if chunk == 1 else t0_ref).at[:, block]

    z, x, core = me // 8, lax.rem(me // 2, 4), lax.rem(me, 2)
    steps = [(dz, dx, dc) for dz in (2, 1, 3, 0) for dx in (2, 1, 3, 0) for dc in (0, 1)]
    steps.sort(key=lambda d: -min(d[0], 4 - d[0]) - min(d[1], 4 - d[1]))
    peers = [
        lax.rem(z + dz, 4) * 8 + lax.rem(x + dx, 4) * 2 + lax.rem(core + dc, 2)
        for dz, dx, dc in steps
        if dz or dx or dc
    ]

    def own_copy(chunk):
        first, tiles = SENT[chunk]
        return pltpu.make_async_copy(
            w_ref.at[me, pl.ds(first, tiles)], landing(chunk, row).at[:, me], own_sem.at[chunk]
        )

    def turn(chunk):
        first, tiles = SENT[chunk]
        for f in peers:
            pltpu.make_async_remote_copy(
                src_ref=w_ref.at[f, pl.ds(first, tiles)], dst_ref=landing(chunk, row).at[:, me],
                send_sem=turn_send.at[chunk], recv_sem=turn_recv.at[chunk, my_half], device_id={"freq": f},
            ).start()
        own_copy(chunk).start()

    my_half = me // (n_freq // 2)
    early = my_half == 0
    late = my_half == 1

    def turn_bytes(chunk, half, count):
        first, tiles = SENT[chunk]
        block = w_ref.at[pl.ds(0, count), pl.ds(first, tiles)]
        return pltpu.make_async_remote_copy(
            src_ref=block, dst_ref=block, send_sem=turn_send.at[chunk], recv_sem=turn_recv.at[chunk, half],
            device_id={"freq": me},
        )

    def turned(chunk, half):
        @pl.when(my_half == half)
        def _():
            turn_bytes(chunk, half, n_freq // 2 - 1).wait_recv()
            own_copy(chunk).wait()

        @pl.when(my_half != half)
        def _():
            turn_bytes(chunk, half, n_freq // 2).wait_recv()

    def part(k, half):
        size = n_freq // 4 if k == 3 else n_freq // 2
        return pl.ds(half * size, size)

    def piece(k, block, half):
        if k > 1:
            return (end_out if k == 2 else x4_out).at[block, part(k, half)]
        return landing(k, block).at[:, part(k, half)]

    def side_copy(k, way, half):
        to = piece(k, row, half)
        ref = to if k < 2 else (end_ref.at[0] if k == 2 else x4_ref).at[part(k, half)]
        return pltpu.make_async_remote_copy(
            src_ref=ref, dst_ref=to, send_sem=side_send.at[k, way, half], recv_sem=side_recv.at[k, way, half],
            device_id={"pair": right if way == 0 else left},
        )

    def pass_copy(k, way):
        ref = piece(k, left if way == 0 else right, way)
        return pltpu.make_async_remote_copy(
            src_ref=ref, dst_ref=ref, send_sem=pass_send.at[k, way], recv_sem=pass_recv.at[k, way],
            device_id={"pair": right if way == 0 else left},
        )

    def spread(half, *pieces):
        for k in pieces:
            for way in range(2):
                side_copy(k, way, half).start()

    def forward(way, *pieces):
        for k in pieces:
            side_copy(k, way, way).wait_recv()
            pass_copy(k, way).start()

    def arrived(*pieces):
        for k in pieces:
            for way in range(2):
                side_copy(k, way, 1 - way).wait_recv()

    def passed(*pieces):
        for k in pieces:
            for way in range(2):
                pass_copy(k, way).wait_recv()

    low = lax.broadcasted_iota(jnp.int32, (INPUTS, LANES), 1) < 64
    real_slot = (lax.broadcasted_iota(jnp.int32, (INPUTS, LANES), 1) & 32) == 0
    zero = jnp.zeros((INPUTS, LANES), jnp.bfloat16)

    def sort(block):
        def one(src, carry):
            t0, t1 = t0_ref[0, block, src], mid_ref[0, block, src]
            x_ref[0, block, src] = jnp.where(low, t0, pltpu.roll(t1, 64, 1))
            x_ref[1, block, src] = jnp.where(low, pltpu.roll(t0, 64, 1), t1)
            return carry

        lax.fori_loop(0, n_freq, one, 0, unroll=4)

    def keep(k, block=0):
        if k == 0:
            pair = x_ref.at[:, block], x_out.at[:, block]
        elif k == 1:
            pair = mid_ref.at[1, block], mid_out.at[block]
        elif k == 2:
            pair = end_ref.at[0], end_out.at[row]
        else:
            pair = (x4_ref, x4_out.at[row]) if k == 3 else (l_ref, l_out)
        return pltpu.make_async_copy(*pair, out_sem.at[k, block])

    def put_rows(c, k, src, x):
        turned_x = jnp.where(real_slot, pltpu.roll(x, 96, 1), -pltpu.roll(x, 32, 1))
        l_ref[c, 0, src, :, k * LANES : (k + 1) * LANES] = x
        l_ref[c, 1, src, :, k * LANES : (k + 1) * LANES] = turned_x

    def rows_early():
        def one(src, carry):
            for c in range(4):
                put_rows(c, 0, src, x_ref[c, row, src] if c < 2 else mid_ref[1, row, src])
            return carry

        lax.fori_loop(0, n_freq, one, 0)

    def rows_late():
        def one(src, carry):
            t3, t4 = end_ref[0, src], end_ref[1, src]
            put_rows(0, 1, src, jnp.where(low, t3, zero))
            put_rows(1, 1, src, jnp.where(low, zero, t3))
            put_rows(2, 1, src, jnp.where(low, t4, zero))
            put_rows(3, 1, src, jnp.where(low, zero, t4))
            return carry

        lax.fori_loop(0, n_freq, one, 0)

    def turn_and_spread(chunk, half):
        turned(chunk, half)
        if chunk == 2:
            for j in range(n_freq // 4):
                src = half * n_freq // 2 + j
                x4_ref[half * n_freq // 4 + j] = jnp.where(low, end_ref[1, src], end_ref[1, src + n_freq // 4])
            spread(half, 2, 3)
        else:
            spread(half, chunk)

    def finish(block):
        sort(block)
        keep(0, block).start()
        keep(1, block).start()

    take = functools.partial(functools.partial, turn_and_spread)
    channelize(0)
    order_gains()
    rearrange(0)
    pl.semaphore_wait(barrier, n_freq + 1)
    turn(0)
    channelize(1, [(1, late, take(0, 0)), (3, late, take(0, 1))])
    pl.when(early)(take(0, 0))
    rearrange(1)
    turn(1)
    pl.when(early)(take(0, 1))

    def between():
        forward(0, 0)
        forward(1, 0)
        turn_and_spread(1, 0)

    channelize(2, [(2, late, between), (3, late, take(1, 1)), (2, early, lambda: forward(0, 0))])

    @pl.when(early)
    def _():
        forward(1, 0)
        turn_and_spread(1, 0)

    rearrange(2)
    turn(2)
    pl.when(early)(take(1, 1))
    finish(row)
    rows_early()
    turn_and_spread(2, 0)
    forward(0, 1)
    turn_and_spread(2, 1)
    forward(1, 1)
    keep(2).start()
    keep(3).start()
    rows_late()
    keep(4).start()
    arrived(0, 1)
    forward(0, 2, 3)
    finish(right)
    finish(left)
    forward(1, 2, 3)
    passed(0, 1)
    finish(lax.rem(row + 2, n_pair))
    arrived(2, 3)
    for k in range(4):
        for way in range(2):
            for half in range(2):
                side_copy(k, way, half).wait_send()
            pass_copy(k, way).wait_send()
    for chunk in range(CHUNKS):
        turn_bytes(chunk, 0, n_freq - 1).wait_send()
    for k in range(5):
        for block in range(n_pair if k < 2 else 1):
            keep(k, block).wait()
    passed(2, 3)


def spectra_call(n_freq, n_pair, voltages, taps_table, dft, gains):
    bf16 = jnp.bfloat16
    anywhere = pl.BlockSpec(memory_space=pl.ANY)
    dma = pltpu.SemaphoreType.DMA
    in_hbm = functools.partial(pltpu.with_memory_space_constraint, memory_space=pltpu.HBM)
    return pl.pallas_call(
        functools.partial(spectra_kernel, n_freq, n_pair),
        out_shape=(
            pltpu.VMEM((2, n_pair, n_freq, INPUTS, LANES), bf16),
            pltpu.VMEM((n_pair, n_freq, INPUTS, LANES), bf16),
            pltpu.VMEM((n_pair, n_freq, INPUTS, LANES), bf16),
            pltpu.VMEM((n_pair, n_freq // 2, INPUTS, LANES), bf16),
            pltpu.VMEM((4, 2, n_freq, INPUTS, 2 * LANES), bf16),
        ),
        in_specs=[anywhere] * 4,
        out_specs=(anywhere,) * 5,
        scratch_shapes=[
            pltpu.VMEM((FRAMES, INPUTS, NFFT), jnp.int32),
            pltpu.VMEM((INPUTS, CHANNELS), jnp.float32),
            pltpu.VMEM((TAPS, NFFT), jnp.float32),
            pltpu.VMEM((TAPS, NFFT // LANES, 8, LANES), jnp.float32),
            pltpu.VMEM((NFFT, 2 * LANES), bf16),
            pltpu.VMEM((INPUTS, 2 * LANES), jnp.float32),
            pltpu.VMEM((SPECTRA * INPUTS, 2 * LANES), bf16),
            pltpu.VMEM((SPECTRA * INPUTS, 2 * LANES), bf16),
            pltpu.VMEM((SPECTRA * INPUTS, 2 * LANES), jnp.float32),
            pltpu.VMEM((SPECTRA * INPUTS, LANES), jnp.float32),
            pltpu.VMEM((n_freq, 5, INPUTS, LANES), bf16),
            pltpu.VMEM((1, n_pair, n_freq, INPUTS, LANES), bf16),
            pltpu.VMEM((2, n_pair, n_freq, INPUTS, LANES), bf16),
            pltpu.VMEM((2, n_pair, n_freq, INPUTS, LANES), bf16),
            pltpu.VMEM((2, n_freq, INPUTS, LANES), bf16),
            pltpu.VMEM((n_freq // 2, INPUTS, LANES), bf16),
            pltpu.VMEM((4, 2, n_freq, INPUTS, 2 * LANES), bf16),
            dma((6,)), dma((3,)), dma((CHUNKS,)), dma((CHUNKS, 2)), dma((CHUNKS,)), dma((5, n_pair)),
            dma((4, 2, 2)), dma((4, 2, 2)), dma((4, 2)), dma((4, 2)),
        ],
        compiler_params=pltpu.CompilerParams(
            collective_id=0, has_side_effects=True, vmem_limit_bytes=VMEM_LIMIT
        ),
    )(*map(in_hbm, (voltages, taps_table, dft, gains)))


def correlate_kernel(n_freq, n_pair, x_ref, mid_ref, end_ref, x4_ref, l_ref, out_hbm, out_buf, sem):
    rows, half = n_freq * INPUTS, n_freq * INPUTS // 2

    def copy(c, p):
        cols = pl.ds(pl.multiple_of(p * rows, rows), rows)
        return pltpu.make_async_copy(out_buf.at[c, p], out_hbm.at[c, :, :, cols], sem.at[c, p])

    for c in range(3):

        def block(p, carry):
            for h in range(2):
                quarters = (2 * h, 2 * h + 1) if c < 2 else (h, h + 2)
                spans = [slice(q * n_freq // 4, (q + 1) * n_freq // 4) for q in quarters]
                if c < 2:
                    first, last = ([ref[p, at] for at in spans] for ref in (x_ref.at[c], end_ref))
                    last = jnp.concatenate(last, 0)
                else:
                    first, last = [mid_ref[p, at] for at in spans], x4_ref[p]
                first = jnp.concatenate(first, 0).reshape(half, LANES)
                side = l_ref[3 if c == 2 and h else c].reshape(2 * rows, 2 * LANES)
                sums = lax.dot_general(
                    side, jnp.concatenate([first, last.reshape(half, LANES)], 1), (((1,), (1,)), ((), ())),
                    preferred_element_type=jnp.float32,
                )
                sums = (sums * (1.0 / SAMPLES)).astype(jnp.bfloat16)
                wide = half // 2
                for k, q in enumerate(quarters):
                    part = sums[:, k * wide : (k + 1) * wide]
                    out_buf[c, p, 0, :, q * wide : (q + 1) * wide] = part[:rows]
                    out_buf[c, p, 1, :, q * wide : (q + 1) * wide] = part[rows:]
            copy(c, p).start()
            return carry

        lax.fori_loop(0, n_pair, block, 0, unroll=True)

    for c in range(3):
        for p in range(n_pair):
            copy(c, p).wait()


def correlate_call(n_freq, n_pair, *spectra):
    rows, columns = n_freq * INPUTS, n_pair * n_freq * INPUTS
    vmem = pl.BlockSpec(memory_space=pltpu.VMEM)
    return pl.pallas_call(
        functools.partial(correlate_kernel, n_freq, n_pair),
        out_shape=jax.ShapeDtypeStruct((3, 2, rows, columns), jnp.bfloat16),
        in_specs=[vmem] * 5,
        out_specs=pl.BlockSpec(memory_space=pl.ANY),
        scratch_shapes=[
            pltpu.VMEM((3, n_pair, 2, rows, rows), jnp.bfloat16),
            pltpu.SemaphoreType.DMA((3, n_pair)),
        ],
        compiler_params=pltpu.CompilerParams(vmem_limit_bytes=VMEM_LIMIT),
    )(*(pltpu.with_memory_space_constraint(x, pltpu.VMEM) for x in spectra))


def solution(mesh):
    n_freq, n_pair = mesh.shape["freq"], mesh.shape["pair"]
    taps_table = jnp.asarray(filter_table())
    dft = jnp.asarray(dft_table()).astype(jnp.bfloat16)

    def body(voltages, gains):
        frames = voltages.transpose(1, 0, 2)
        return correlate_call(n_freq, n_pair, *spectra_call(n_freq, n_pair, frames, taps_table, dft, gains))

    placed = (P(("pair", "freq"), None, None), P(("pair", "freq"), None))
    return jax.shard_map(
        body, mesh=mesh, in_specs=placed, out_specs=P("freq", None, "pair", None), check_vma=False
    )
```

```python
import functools
import math

import jax
import jax.numpy as jnp
import numpy as np
from jax import lax
from jax.experimental import pallas as pl
from jax.experimental.pallas import tpu as pltpu
from jax.sharding import PartitionSpec as P

NFFT = 2048
TAPS = 8
SAMPLES = 96
FRAMES = 103
FIRST = 256
CHANNELS = 96
CHUNKS = 3
SPECTRA = SAMPLES // CHUNKS
INPUTS = 16
LANES = 128
GROUPS = ((0, 0), (0, 1), (1, 0), (1, 1), (2, 0), (2, 1), (2, 0), (2, 1))
SENT = ((0, 2), (2, 1), (3, 2))
VMEM_LIMIT = 36 * 1024 * 1024


def filter_table():
    positions = np.arange(TAPS * NFFT, dtype=np.float64)
    span_width = float(TAPS * NFFT)
    window = 0.5 - 0.5 * np.cos(2.0 * np.pi * (positions + 0.5) / span_width)
    taps_table = window * np.sinc((positions - span_width / 2 + 0.5) / NFFT)
    return taps_table.astype(np.float32).reshape(TAPS, NFFT)


def dft_table():
    samples = np.arange(NFFT)
    bins = FIRST + np.arange(CHANNELS)
    angles = (bins[:, None] * samples[None, :] % NFFT) * (2.0 * math.pi / NFFT)
    amplitude = 0.25 / math.sqrt(NFFT)
    tables = np.stack([np.cos(angles) * amplitude, -np.sin(angles) * amplitude])
    columns = [tables[part, channel::3] for channel, part in GROUPS]
    return np.concatenate(columns, 0).T.astype(np.float32)


def exchange_lanes(rows):
    lane = lax.broadcasted_iota(jnp.int32, rows[0].shape, 1)
    step = len(rows) // 2
    while step:
        odd = (lane & step) != 0
        out = list(rows)
        for s in range(len(rows)):
            if not s & step:
                low, high = rows[s], rows[s + step]
                out[s] = jnp.where(odd, pltpu.roll(high, step, 1), low)
                out[s + step] = jnp.where(odd, high, pltpu.roll(low, LANES - step, 1))
        rows, step = out, step // 2
    return rows


def spectra_kernel(
    n_freq, n_pair, v_hbm, taps_hbm, dft_hbm, gains_hbm, x_out, mid_out, end_out, x4_out, l_out,
    v_buf, gains_ref, taps_raw, taps_buf, dft_buf, gain_buf, f0, f1, y_ref, c2_ref, w_ref, t0_ref, x_ref, mid_ref, end_ref, x4_ref, l_ref,
    v_sem, table_sem, turn_send, turn_recv, own_sem, out_sem, side_send, side_recv, pass_send, pass_recv,
):
    me = lax.axis_index("freq")
    row = lax.axis_index("pair")
    right, left = lax.rem(row + 1, n_pair), lax.rem(row + n_pair - 1, n_pair)

    tables = [
        pltpu.make_async_copy(taps_hbm, taps_raw, table_sem.at[0]),
        pltpu.make_async_copy(dft_hbm, dft_buf, table_sem.at[1]),
        pltpu.make_async_copy(gains_hbm, gains_ref, table_sem.at[2]),
    ]
    tables[0].start()
    history = TAPS - 1

    def first_load(piece):
        frames = pl.ds(0, SPECTRA + history)
        cols = pl.ds(pl.multiple_of(piece * (NFFT // 4), NFFT // 4), NFFT // 4)
        return pltpu.make_async_copy(
            v_hbm.at[frames, :, cols], v_buf.at[frames, :, cols], v_sem.at[piece]
        )

    def later_load(chunk):
        frames = pl.ds(chunk * SPECTRA + history, SPECTRA)
        return pltpu.make_async_copy(v_hbm.at[frames], v_buf.at[frames], v_sem.at[3 + chunk])

    first_load(0).start()
    tables[1].start()
    tables[2].start()
    first_load(1).start()

    barrier = pltpu.get_barrier_semaphore()

    def greet(j, carry):
        pl.semaphore_signal(barrier, inc=1, device_id={"freq": lax.rem(me + j, n_freq)})
        return carry

    lax.fori_loop(1, n_freq, greet, 0)
    for side in (left, right):
        pl.semaphore_signal(barrier, inc=1, device_id={"pair": side})

    tables[0].wait()
    for t in range(TAPS):
        for n in range(NFFT // LANES):
            taps_buf[t, n] = jnp.broadcast_to(
                taps_raw[t : t + 1, n * LANES : (n + 1) * LANES], (8, LANES)
            )

    def filter_slice(chunk, q, out):
        for u in range(2):
            n = 2 * q + u
            col = pl.ds(pl.multiple_of(n * LANES, LANES), LANES)
            taps = [taps_buf[t, n] for t in range(TAPS)]

            def frame(s, half):
                return v_buf[chunk * SPECTRA + s, half * 8 : half * 8 + 8, col].astype(jnp.float32)

            window = [[frame(s, half) for s in range(TAPS)] for half in range(2)]
            for s in range(SPECTRA):
                halves = []
                for half in range(2):
                    if s > 0:
                        window[half] = window[half][1:] + [frame(s + TAPS - 1, half)]
                    terms = [taps[t] * window[half][t] for t in range(TAPS)]
                    while len(terms) > 1:
                        terms = [a + b for a, b in zip(terms[::2], terms[1::2])]
                    halves.append(terms[0])
                out[s * INPUTS : (s + 1) * INPUTS, u * LANES : (u + 1) * LANES] = jnp.concatenate(
                    halves, 0
                ).astype(jnp.bfloat16)

    def transform_slice(q, filtered, start=False):
        rows = pl.ds(pl.multiple_of(q * 2 * LANES, 2 * LANES), 2 * LANES)
        part = jnp.dot(filtered[...], dft_buf[rows, :], preferred_element_type=jnp.float32)
        if start:
            y_ref[...] = part
        else:
            y_ref[...] += part

    def channelize(chunk, serve=()):
        if chunk == 0:
            first_load(0).wait()
            first_load(2).start()
        else:
            later_load(chunk).wait()
        if chunk == 1:
            later_load(2).start()
        filter_slice(chunk, 0, f0)
        if chunk == 0:
            tables[1].wait()
        transform_slice(0, f0, True)
        filter_slice(chunk, 1, f1)

        def step(j, carry):
            if chunk == 0:
                first_load(j).wait()
                pl.when(j == 1)(lambda: first_load(3).start())
                pl.when(j == 2)(lambda: later_load(1).start())
            for when, who, what in serve:
                pl.when((j == when) & who)(what)
            transform_slice(2 * j - 1, f1)
            filter_slice(chunk, 2 * j, f0)
            transform_slice(2 * j, f0)
            filter_slice(chunk, 2 * j + 1, f1)
            return carry

        lax.fori_loop(1, NFFT // LANES // 4, step, 0)
        transform_slice(NFFT // LANES // 2 - 1, f1)

    def order_gains():
        tables[2].wait()
        lane = lax.broadcasted_iota(jnp.int32, (CHANNELS, 2 * LANES), 1)
        chan = lax.broadcasted_iota(jnp.int32, (CHANNELS, 2 * LANES), 0)
        wanted = 3 * (lane % 32) + jnp.minimum(lane // 64, 2)
        picks = jnp.where(chan == wanted, 1.0, 0.0).astype(jnp.float32)
        gain_buf[...] = jnp.dot(
            gains_ref[...], picks, precision=lax.Precision.HIGHEST, preferred_element_type=jnp.float32
        )

    def rearrange(chunk):
        def spread(rows, tile):
            for f, block in enumerate(exchange_lanes(rows)):
                w_ref[f, tile] = block

        tile = SENT[chunk][0]
        at = [slice(s * INPUTS, (s + 1) * INPUTS) for s in range(SPECTRA)]
        spread([(y_ref[r, :LANES] * gain_buf[:, :LANES]).astype(jnp.bfloat16) for r in at], tile)
        if chunk == 1:
            c2_ref[...] = y_ref[:, LANES:]
            return
        lane = lax.broadcasted_iota(jnp.int32, (INPUTS, LANES), 1)
        rows = []
        for r in at:
            part = y_ref[r, LANES:]
            if chunk == 2:
                part = jnp.where(lane < 64, c2_ref[r, :], part)
            rows.append((part * gain_buf[:, LANES:]).astype(jnp.bfloat16))
        spread(rows, tile + 1)

    def landing(chunk, block):
        if chunk == 2:
            return end_ref
        return (mid_ref if chunk == 1 else t0_ref).at[:, block]

    z, x, core = me // 8, lax.rem(me // 2, 4), lax.rem(me, 2)
    steps = [(dz, dx, dc) for dz in (2, 1, 3, 0) for dx in (2, 1, 3, 0) for dc in (0, 1)]
    steps.sort(key=lambda d: -min(d[0], 4 - d[0]) - min(d[1], 4 - d[1]))
    peers = [
        lax.rem(z + dz, 4) * 8 + lax.rem(x + dx, 4) * 2 + lax.rem(core + dc, 2)
        for dz, dx, dc in steps
        if dz or dx or dc
    ]

    def own_copy(chunk):
        first, tiles = SENT[chunk]
        return pltpu.make_async_copy(
            w_ref.at[me, pl.ds(first, tiles)], landing(chunk, row).at[:, me], own_sem.at[chunk]
        )

    def turn(chunk):
        first, tiles = SENT[chunk]
        for f in peers:
            pltpu.make_async_remote_copy(
                src_ref=w_ref.at[f, pl.ds(first, tiles)], dst_ref=landing(chunk, row).at[:, me],
                send_sem=turn_send.at[chunk], recv_sem=turn_recv.at[chunk, my_half], device_id={"freq": f},
            ).start()
        own_copy(chunk).start()

    my_half = me // (n_freq // 2)
    early = my_half == 0
    late = my_half == 1

    def turn_bytes(chunk, half, count):
        first, tiles = SENT[chunk]
        block = w_ref.at[pl.ds(0, count), pl.ds(first, tiles)]
        return pltpu.make_async_remote_copy(
            src_ref=block, dst_ref=block, send_sem=turn_send.at[chunk], recv_sem=turn_recv.at[chunk, half],
            device_id={"freq": me},
        )

    def turned(chunk, half):
        @pl.when(my_half == half)
        def _():
            turn_bytes(chunk, half, n_freq // 2 - 1).wait_recv()
            own_copy(chunk).wait()

        @pl.when(my_half != half)
        def _():
            turn_bytes(chunk, half, n_freq // 2).wait_recv()

    def part(k, quarter):
        size = n_freq // 8 if k == 3 else n_freq // 4
        return pl.ds(quarter * size, size)

    def piece(k, block, quarter):
        ref = (t0_ref.at[0], mid_ref.at[0], end_out, x4_out, mid_out)[k]
        return ref.at[block, part(k, quarter)]

    def side_copy(k, way, quarter):
        to = piece(k, row, quarter)
        ref = to if k < 2 else (end_ref.at[0], x4_ref, end_ref.at[1])[k - 2].at[part(k, quarter)]
        return pltpu.make_async_remote_copy(
            src_ref=ref, dst_ref=to, send_sem=side_send.at[k, way, quarter], recv_sem=side_recv.at[k, way, quarter],
            device_id={"pair": right if way == 0 else left},
        )

    def pass_copy(k, way, half):
        ref = piece(k, left if way == 0 else right, 2 * half + way)
        return pltpu.make_async_remote_copy(
            src_ref=ref, dst_ref=ref, send_sem=pass_send.at[k, way, half], recv_sem=pass_recv.at[k, way, half],
            device_id={"pair": right if way == 0 else left},
        )

    def spread(half, handed_on, *pieces):
        for k in pieces:
            for way in range(2):
                side_copy(k, way, 2 * half + (way if handed_on else 1 - way)).start()

    def forward(half, *pieces):
        for k in pieces:
            for way in range(2):
                side_copy(k, way, 2 * half + way).wait_recv()
                pass_copy(k, way, half).start()

    def arrived(*pieces):
        for k in pieces:
            for way in range(2):
                for half in range(2):
                    side_copy(k, way, 2 * half + 1 - way).wait_recv()

    def passed(*pieces):
        for k in pieces:
            for way in range(2):
                for half in range(2):
                    pass_copy(k, way, half).wait_recv()

    low = lax.broadcasted_iota(jnp.int32, (INPUTS, LANES), 1) < 64
    real_slot = (lax.broadcasted_iota(jnp.int32, (INPUTS, LANES), 1) & 32) == 0
    zero = jnp.zeros((INPUTS, LANES), jnp.bfloat16)

    def sort(block):
        def one(src, carry):
            t0, t1 = t0_ref[0, block, src], mid_ref[0, block, src]
            x_ref[0, block, src] = jnp.where(low, t0, pltpu.roll(t1, 64, 1))
            x_ref[1, block, src] = jnp.where(low, pltpu.roll(t0, 64, 1), t1)
            return carry

        lax.fori_loop(0, n_freq, one, 0, unroll=8)

    def keep(k, block=0):
        if k == 0:
            pair = x_ref.at[:, block], x_out.at[:, block]
        elif k == 1:
            pair = end_ref.at[1], mid_out.at[row]
        elif k == 2:
            pair = end_ref.at[0], end_out.at[row]
        else:
            pair = (x4_ref, x4_out.at[row]) if k == 3 else (l_ref, l_out)
        return pltpu.make_async_copy(*pair, out_sem.at[k, block])

    def put_rows(c, k, src, x):
        turned_x = jnp.where(real_slot, pltpu.roll(x, 96, 1), -pltpu.roll(x, 32, 1))
        l_ref[c, 0, src, :, k * LANES : (k + 1) * LANES] = x
        l_ref[c, 1, src, :, k * LANES : (k + 1) * LANES] = turned_x

    def rows_early():
        def one(src, carry):
            for c in range(2):
                put_rows(c, 0, src, x_ref[c, row, src])
            t1 = t0_ref[1, row, src]
            put_rows(2, 1, src, jnp.where(low, t1, zero))
            put_rows(3, 1, src, jnp.where(low, zero, t1))
            return carry

        lax.fori_loop(0, n_freq, one, 0, unroll=8)

    def rows_late():
        def one(src, carry):
            t3, t4 = end_ref[0, src], end_ref[1, src]
            put_rows(0, 1, src, jnp.where(low, t3, zero))
            put_rows(1, 1, src, jnp.where(low, zero, t3))
            put_rows(2, 0, src, t4)
            put_rows(3, 0, src, t4)
            return carry

        lax.fori_loop(0, n_freq, one, 0, unroll=8)

    def turn_and_spread(chunk, half):
        turned(chunk, half)
        if chunk == 2:
            spread(half, True, 2, 4)
        elif chunk == 1:
            spread(half, True, 1)
            spread(half, False, 1)
        else:
            spread(half, True, 0)
            for j in range(n_freq // 4):
                src = half * n_freq // 2 + j
                pair = t0_ref[1, row, src], t0_ref[1, row, src + n_freq // 4]
                x4_ref[half * n_freq // 4 + j] = jnp.where(low, *pair)
            spread(half, True, 3)
            spread(half, False, 0, 3)

    def finish(block):
        sort(block)
        keep(0, block).start()

    take = functools.partial(functools.partial, turn_and_spread)
    channelize(0)
    order_gains()
    rearrange(0)
    pl.semaphore_wait(barrier, n_freq + 1)
    turn(0)
    channelize(1, [(1, late, take(0, 0)), (3, late, take(0, 1))])
    pl.when(early)(take(0, 0))
    rearrange(1)
    turn(1)
    pl.when(early)(take(0, 1))
    pl.when(late)(lambda: forward(0, 0, 3))

    def between():
        forward(1, 0, 3)
        turn_and_spread(1, 0)

    channelize(2, [(2, late, between), (3, late, take(1, 1)), (2, early, lambda: forward(0, 0, 3))])

    @pl.when(early)
    def _():
        forward(1, 0, 3)
        turn_and_spread(1, 0)

    rearrange(2)
    turn(2)
    pl.when(early)(take(1, 1))
    forward(0, 1)
    turn_and_spread(2, 0)
    spread(0, False, 2, 4)
    forward(1, 1)
    turn_and_spread(2, 1)
    spread(1, False, 2, 4)
    finish(row)
    rows_early()
    keep(1).start()
    keep(2).start()
    keep(3).start()
    rows_late()
    keep(4).start()
    arrived(0, 1, 3)
    finish(right)
    forward(0, 2, 4)
    finish(left)
    forward(1, 2, 4)
    passed(0, 1, 3)
    finish(lax.rem(row + 2, n_pair))
    arrived(2, 4)
    for k in range(5):
        for way in range(2):
            for quarter in range(4):
                side_copy(k, way, quarter).wait_send()
            for half in range(2):
                pass_copy(k, way, half).wait_send()
    for chunk in range(CHUNKS):
        turn_bytes(chunk, 0, n_freq - 1).wait_send()
    for k in range(5):
        for block in range(n_pair if k == 0 else 1):
            keep(k, block).wait()
    passed(2, 4)


def spectra_call(n_freq, n_pair, voltages, taps_table, dft, gains):
    bf16 = jnp.bfloat16
    anywhere = pl.BlockSpec(memory_space=pl.ANY)
    dma = pltpu.SemaphoreType.DMA
    in_hbm = functools.partial(pltpu.with_memory_space_constraint, memory_space=pltpu.HBM)
    return pl.pallas_call(
        functools.partial(spectra_kernel, n_freq, n_pair),
        out_shape=(
            pltpu.VMEM((2, n_pair, n_freq, INPUTS, LANES), bf16),
            pltpu.VMEM((n_pair, n_freq, INPUTS, LANES), bf16),
            pltpu.VMEM((n_pair, n_freq, INPUTS, LANES), bf16),
            pltpu.VMEM((n_pair, n_freq // 2, INPUTS, LANES), bf16),
            pltpu.VMEM((4, 2, n_freq, INPUTS, 2 * LANES), bf16),
        ),
        in_specs=[anywhere] * 4,
        out_specs=(anywhere,) * 5,
        scratch_shapes=[
            pltpu.VMEM((FRAMES, INPUTS, NFFT), jnp.int32),
            pltpu.VMEM((INPUTS, CHANNELS), jnp.float32),
            pltpu.VMEM((TAPS, NFFT), jnp.float32),
            pltpu.VMEM((TAPS, NFFT // LANES, 8, LANES), jnp.float32),
            pltpu.VMEM((NFFT, 2 * LANES), bf16),
            pltpu.VMEM((INPUTS, 2 * LANES), jnp.float32),
            pltpu.VMEM((SPECTRA * INPUTS, 2 * LANES), bf16),
            pltpu.VMEM((SPECTRA * INPUTS, 2 * LANES), bf16),
            pltpu.VMEM((SPECTRA * INPUTS, 2 * LANES), jnp.float32),
            pltpu.VMEM((SPECTRA * INPUTS, LANES), jnp.float32),
            pltpu.VMEM((n_freq, 5, INPUTS, LANES), bf16),
            pltpu.VMEM((2, n_pair, n_freq, INPUTS, LANES), bf16),
            pltpu.VMEM((2, n_pair, n_freq, INPUTS, LANES), bf16),
            pltpu.VMEM((1, n_pair, n_freq, INPUTS, LANES), bf16),
            pltpu.VMEM((2, n_freq, INPUTS, LANES), bf16),
            pltpu.VMEM((n_freq // 2, INPUTS, LANES), bf16),
            pltpu.VMEM((4, 2, n_freq, INPUTS, 2 * LANES), bf16),
            dma((6,)), dma((3,)), dma((CHUNKS,)), dma((CHUNKS, 2)), dma((CHUNKS,)), dma((5, n_pair)),
            dma((5, 2, 4)), dma((5, 2, 4)), dma((5, 2, 2)), dma((5, 2, 2)),
        ],
        compiler_params=pltpu.CompilerParams(
            collective_id=0, has_side_effects=True, vmem_limit_bytes=VMEM_LIMIT
        ),
    )(*map(in_hbm, (voltages, taps_table, dft, gains)))


def correlate_kernel(n_freq, n_pair, x_ref, mid_ref, end_ref, x4_ref, l_ref, out_hbm, out_buf, sem):
    rows, half = n_freq * INPUTS, n_freq * INPUTS // 2

    def copy(c, p):
        cols = pl.ds(pl.multiple_of(p * rows, rows), rows)
        return pltpu.make_async_copy(out_buf.at[c, p], out_hbm.at[c, :, :, cols], sem.at[c, p])

    for c in range(3):

        def block(p, carry):
            for h in range(2):
                quarters = (2 * h, 2 * h + 1) if c < 2 else (h, h + 2)
                spans = [slice(q * n_freq // 4, (q + 1) * n_freq // 4) for q in quarters]
                if c < 2:
                    first, last = ([ref[p, at] for at in spans] for ref in (x_ref.at[c], end_ref))
                    last = jnp.concatenate(last, 0)
                else:
                    first, last = [mid_ref[p, at] for at in spans], x4_ref[p]
                first = jnp.concatenate(first, 0).reshape(half, LANES)
                side = l_ref[3 if c == 2 and h else c].reshape(2 * rows, 2 * LANES)
                sums = lax.dot_general(
                    side, jnp.concatenate([first, last.reshape(half, LANES)], 1), (((1,), (1,)), ((), ())),
                    preferred_element_type=jnp.float32,
                )
                sums = (sums * (1.0 / SAMPLES)).astype(jnp.bfloat16)
                wide = half // 2
                for k, q in enumerate(quarters):
                    part = sums[:, k * wide : (k + 1) * wide]
                    out_buf[c, p, 0, :, q * wide : (q + 1) * wide] = part[:rows]
                    out_buf[c, p, 1, :, q * wide : (q + 1) * wide] = part[rows:]
            copy(c, p).start()
            return carry

        lax.fori_loop(0, n_pair, block, 0, unroll=True)

    for c in range(3):
        for p in range(n_pair):
            copy(c, p).wait()


def correlate_call(n_freq, n_pair, *spectra):
    rows, columns = n_freq * INPUTS, n_pair * n_freq * INPUTS
    vmem = pl.BlockSpec(memory_space=pltpu.VMEM)
    return pl.pallas_call(
        functools.partial(correlate_kernel, n_freq, n_pair),
        out_shape=jax.ShapeDtypeStruct((3, 2, rows, columns), jnp.bfloat16),
        in_specs=[vmem] * 5,
        out_specs=pl.BlockSpec(memory_space=pl.ANY),
        scratch_shapes=[
            pltpu.VMEM((3, n_pair, 2, rows, rows), jnp.bfloat16),
            pltpu.SemaphoreType.DMA((3, n_pair)),
        ],
        compiler_params=pltpu.CompilerParams(vmem_limit_bytes=VMEM_LIMIT),
    )(*(pltpu.with_memory_space_constraint(x, pltpu.VMEM) for x in spectra))


def solution(mesh):
    n_freq, n_pair = mesh.shape["freq"], mesh.shape["pair"]
    taps_table = jnp.asarray(filter_table())
    dft = jnp.asarray(dft_table()).astype(jnp.bfloat16)

    def body(voltages, gains):
        frames = voltages.transpose(1, 0, 2)
        return correlate_call(n_freq, n_pair, *spectra_call(n_freq, n_pair, frames, taps_table, dft, gains))

    placed = (P(("pair", "freq"), None, None), P(("pair", "freq"), None))
    return jax.shard_map(
        body, mesh=mesh, in_specs=placed, out_specs=P("freq", None, "pair", None), check_vma=False
    )
```

```python
import functools
import math

import jax
import jax.numpy as jnp
import numpy as np
from jax import lax
from jax.experimental import pallas as pl
from jax.experimental.pallas import tpu as pltpu
from jax.sharding import PartitionSpec as P

NFFT = 2048
TAPS = 8
SAMPLES = 96
FRAMES = 103
FIRST = 256
CHANNELS = 96
CHUNKS = 3
SPECTRA = SAMPLES // CHUNKS
INPUTS = 16
LANES = 128
GROUPS = ((0, 0), (0, 1), (1, 0), (1, 1), (2, 0), (2, 1), (2, 0), (2, 1))
SENT = ((0, 2), (2, 1), (3, 2))
VMEM_LIMIT = 36 * 1024 * 1024


def filter_table():
    positions = np.arange(TAPS * NFFT, dtype=np.float64)
    span_width = float(TAPS * NFFT)
    window = 0.5 - 0.5 * np.cos(2.0 * np.pi * (positions + 0.5) / span_width)
    taps_table = window * np.sinc((positions - span_width / 2 + 0.5) / NFFT)
    return taps_table.astype(np.float32).reshape(TAPS, NFFT)


def dft_table():
    samples = np.arange(NFFT)
    bins = FIRST + np.arange(CHANNELS)
    angles = (bins[:, None] * samples[None, :] % NFFT) * (2.0 * math.pi / NFFT)
    amplitude = 0.25 / math.sqrt(NFFT)
    tables = np.stack([np.cos(angles) * amplitude, -np.sin(angles) * amplitude])
    columns = [tables[part, channel::3] for channel, part in GROUPS]
    return np.concatenate(columns, 0).T.astype(np.float32)


def exchange_lanes(rows):
    lane = lax.broadcasted_iota(jnp.int32, rows[0].shape, 1)
    step = len(rows) // 2
    while step:
        odd = (lane & step) != 0
        out = list(rows)
        for s in range(len(rows)):
            if not s & step:
                low, high = rows[s], rows[s + step]
                out[s] = jnp.where(odd, pltpu.roll(high, step, 1), low)
                out[s + step] = jnp.where(odd, high, pltpu.roll(low, LANES - step, 1))
        rows, step = out, step // 2
    return rows


def spectra_kernel(
    n_freq, n_pair, v_hbm, taps_hbm, dft_hbm, gains_hbm, x_out, mid_out, end_out, x4_out, l_out,
    v_buf, gains_ref, taps_raw, taps_buf, dft_buf, gain_buf, f0, f1, y_ref, c2_ref, w_ref, t0_ref, x_ref, mid_ref, end_ref, x4_ref, l_ref,
    v_sem, table_sem, turn_send, turn_recv, own_sem, out_sem, side_send, side_recv, pass_send, pass_recv,
):
    me = lax.axis_index("freq")
    row = lax.axis_index("pair")
    right, left = lax.rem(row + 1, n_pair), lax.rem(row + n_pair - 1, n_pair)

    tables = [
        pltpu.make_async_copy(taps_hbm, taps_raw, table_sem.at[0]),
        pltpu.make_async_copy(dft_hbm, dft_buf, table_sem.at[1]),
        pltpu.make_async_copy(gains_hbm, gains_ref, table_sem.at[2]),
    ]
    tables[0].start()
    history = TAPS - 1

    def first_load(piece):
        frames = pl.ds(0, SPECTRA + history)
        cols = pl.ds(pl.multiple_of(piece * (NFFT // 4), NFFT // 4), NFFT // 4)
        return pltpu.make_async_copy(
            v_hbm.at[frames, :, cols], v_buf.at[frames, :, cols], v_sem.at[piece]
        )

    def later_load(chunk):
        frames = pl.ds(chunk * SPECTRA + history, SPECTRA)
        return pltpu.make_async_copy(v_hbm.at[frames], v_buf.at[frames], v_sem.at[3 + chunk])

    first_load(0).start()
    tables[1].start()
    tables[2].start()
    first_load(1).start()

    barrier = pltpu.get_barrier_semaphore()

    def greet(j, carry):
        pl.semaphore_signal(barrier, inc=1, device_id={"freq": lax.rem(me + j, n_freq)})
        return carry

    lax.fori_loop(1, n_freq, greet, 0)
    for side in (left, right):
        pl.semaphore_signal(barrier, inc=1, device_id={"pair": side})

    tables[0].wait()
    for t in range(TAPS):
        for n in range(NFFT // LANES):
            taps_buf[t, n] = jnp.broadcast_to(
                taps_raw[t : t + 1, n * LANES : (n + 1) * LANES], (8, LANES)
            )

    def filter_slice(chunk, q, out):
        for u in range(2):
            n = 2 * q + u
            col = pl.ds(pl.multiple_of(n * LANES, LANES), LANES)
            taps = [taps_buf[t, n] for t in range(TAPS)]

            def frame(s, half):
                return v_buf[chunk * SPECTRA + s, half * 8 : half * 8 + 8, col].astype(jnp.float32)

            window = [[frame(s, half) for s in range(TAPS)] for half in range(2)]
            for s in range(SPECTRA):
                halves = []
                for half in range(2):
                    if s > 0:
                        window[half] = window[half][1:] + [frame(s + TAPS - 1, half)]
                    terms = [taps[t] * window[half][t] for t in range(TAPS)]
                    while len(terms) > 1:
                        terms = [a + b for a, b in zip(terms[::2], terms[1::2])]
                    halves.append(terms[0])
                out[s * INPUTS : (s + 1) * INPUTS, u * LANES : (u + 1) * LANES] = jnp.concatenate(
                    halves, 0
                ).astype(jnp.bfloat16)

    def transform_slice(q, filtered, start=False):
        rows = pl.ds(pl.multiple_of(q * 2 * LANES, 2 * LANES), 2 * LANES)
        part = jnp.dot(filtered[...], dft_buf[rows, :], preferred_element_type=jnp.float32)
        if start:
            y_ref[...] = part
        else:
            y_ref[...] += part

    def channelize(chunk, serve=()):
        if chunk == 0:
            first_load(0).wait()
            first_load(2).start()
        else:
            later_load(chunk).wait()
        if chunk == 1:
            later_load(2).start()
        filter_slice(chunk, 0, f0)
        if chunk == 0:
            tables[1].wait()
        transform_slice(0, f0, True)
        filter_slice(chunk, 1, f1)

        def step(j, carry):
            if chunk == 0:
                first_load(j).wait()
                pl.when(j == 1)(lambda: first_load(3).start())
                pl.when(j == 2)(lambda: later_load(1).start())
            for when, who, what in serve:
                pl.when((j == when) & who)(what)
            transform_slice(2 * j - 1, f1)
            filter_slice(chunk, 2 * j, f0)
            transform_slice(2 * j, f0)
            filter_slice(chunk, 2 * j + 1, f1)
            return carry

        lax.fori_loop(1, NFFT // LANES // 4, step, 0)
        transform_slice(NFFT // LANES // 2 - 1, f1)

    def order_gains():
        tables[2].wait()
        lane = lax.broadcasted_iota(jnp.int32, (CHANNELS, 2 * LANES), 1)
        chan = lax.broadcasted_iota(jnp.int32, (CHANNELS, 2 * LANES), 0)
        wanted = 3 * (lane % 32) + jnp.minimum(lane // 64, 2)
        picks = jnp.where(chan == wanted, 1.0, 0.0).astype(jnp.float32)
        gain_buf[...] = jnp.dot(
            gains_ref[...], picks, precision=lax.Precision.HIGHEST, preferred_element_type=jnp.float32
        )

    def rearrange(chunk):
        def spread(rows, tile):
            for f, block in enumerate(exchange_lanes(rows)):
                w_ref[f, tile] = block

        tile = SENT[chunk][0]
        at = [slice(s * INPUTS, (s + 1) * INPUTS) for s in range(SPECTRA)]
        spread([(y_ref[r, :LANES] * gain_buf[:, :LANES]).astype(jnp.bfloat16) for r in at], tile)
        if chunk == 1:
            c2_ref[...] = y_ref[:, LANES:]
            return
        lane = lax.broadcasted_iota(jnp.int32, (INPUTS, LANES), 1)
        rows = []
        for r in at:
            part = y_ref[r, LANES:]
            if chunk == 2:
                part = jnp.where(lane < 64, c2_ref[r, :], part)
            rows.append((part * gain_buf[:, LANES:]).astype(jnp.bfloat16))
        spread(rows, tile + 1)

    def landing(chunk, block):
        if chunk == 2:
            return end_ref
        return (mid_ref if chunk == 1 else t0_ref).at[:, block]

    z, x, core = me // 8, lax.rem(me // 2, 4), lax.rem(me, 2)
    steps = [(dz, dx, dc) for dz in (2, 1, 3, 0) for dx in (2, 1, 3, 0) for dc in (0, 1)]
    steps.sort(key=lambda d: -min(d[0], 4 - d[0]) - min(d[1], 4 - d[1]))
    peers = [
        lax.rem(z + dz, 4) * 8 + lax.rem(x + dx, 4) * 2 + lax.rem(core + dc, 2)
        for dz, dx, dc in steps
        if dz or dx or dc
    ]

    def own_copy(chunk):
        first, tiles = SENT[chunk]
        return pltpu.make_async_copy(
            w_ref.at[me, pl.ds(first, tiles)], landing(chunk, row).at[:, me], own_sem.at[chunk]
        )

    def turn(chunk):
        first, tiles = SENT[chunk]
        for f in peers:
            pltpu.make_async_remote_copy(
                src_ref=w_ref.at[f, pl.ds(first, tiles)], dst_ref=landing(chunk, row).at[:, me],
                send_sem=turn_send.at[chunk], recv_sem=turn_recv.at[chunk, my_half], device_id={"freq": f},
            ).start()
        own_copy(chunk).start()

    my_half = me // (n_freq // 2)
    early = my_half == 0
    late = my_half == 1

    def turn_bytes(chunk, half, count):
        first, tiles = SENT[chunk]
        block = w_ref.at[pl.ds(0, count), pl.ds(first, tiles)]
        return pltpu.make_async_remote_copy(
            src_ref=block, dst_ref=block, send_sem=turn_send.at[chunk], recv_sem=turn_recv.at[chunk, half],
            device_id={"freq": me},
        )

    def turned(chunk, half):
        @pl.when(my_half == half)
        def _():
            turn_bytes(chunk, half, n_freq // 2 - 1).wait_recv()
            own_copy(chunk).wait()

        @pl.when(my_half != half)
        def _():
            turn_bytes(chunk, half, n_freq // 2).wait_recv()

    def part(k, quarter):
        size = n_freq // 8 if k == 3 else n_freq // 4
        return pl.ds(quarter * size, size)

    def piece(k, block, quarter):
        ref = (t0_ref.at[0], mid_ref.at[0], end_out, x4_out, mid_out)[k]
        return ref.at[block, part(k, quarter)]

    def side_copy(k, way, quarter):
        to = piece(k, row, quarter)
        ref = to if k < 2 else (end_ref.at[0], x4_ref, end_ref.at[1])[k - 2].at[part(k, quarter)]
        return pltpu.make_async_remote_copy(
            src_ref=ref, dst_ref=to, send_sem=side_send.at[k, way, quarter], recv_sem=side_recv.at[k, way, quarter],
            device_id={"pair": right if way == 0 else left},
        )

    def pass_copy(k, way, half):
        ref = piece(k, left if way == 0 else right, 2 * half + way)
        return pltpu.make_async_remote_copy(
            src_ref=ref, dst_ref=ref, send_sem=pass_send.at[k, way, half], recv_sem=pass_recv.at[k, way, half],
            device_id={"pair": right if way == 0 else left},
        )

    def spread(half, handed_on, *pieces):
        for k in pieces:
            for way in range(2):
                side_copy(k, way, 2 * half + (way if handed_on else 1 - way)).start()

    def forward(half, *pieces):
        for k in pieces:
            for way in range(2):
                side_copy(k, way, 2 * half + way).wait_recv()
                pass_copy(k, way, half).start()

    def arrived(*pieces):
        for k in pieces:
            for way in range(2):
                for half in range(2):
                    side_copy(k, way, 2 * half + 1 - way).wait_recv()

    def passed(*pieces):
        for k in pieces:
            for way in range(2):
                for half in range(2):
                    pass_copy(k, way, half).wait_recv()

    low = lax.broadcasted_iota(jnp.int32, (INPUTS, LANES), 1) < 64
    real_slot = (lax.broadcasted_iota(jnp.int32, (INPUTS, LANES), 1) & 32) == 0
    zero = jnp.zeros((INPUTS, LANES), jnp.bfloat16)

    def sort(block):
        def one(src, carry):
            t0, t1 = t0_ref[0, block, src], mid_ref[0, block, src]
            x_ref[0, block, src] = jnp.where(low, t0, pltpu.roll(t1, 64, 1))
            x_ref[1, block, src] = jnp.where(low, pltpu.roll(t0, 64, 1), t1)
            return carry

        lax.fori_loop(0, n_freq, one, 0, unroll=8)

    def keep(k, block=0):
        if k == 0:
            pair = x_ref.at[:, block], x_out.at[:, block]
        elif k == 1:
            pair = end_ref.at[1], mid_out.at[row]
        elif k == 2:
            pair = end_ref.at[0], end_out.at[row]
        else:
            pair = (x4_ref, x4_out.at[row]) if k == 3 else (l_ref, l_out)
        return pltpu.make_async_copy(*pair, out_sem.at[k, block])

    def put_rows(c, k, src, x):
        turned_x = jnp.where(real_slot, pltpu.roll(x, 96, 1), -pltpu.roll(x, 32, 1))
        l_ref[c, 0, src, :, k * LANES : (k + 1) * LANES] = x
        l_ref[c, 1, src, :, k * LANES : (k + 1) * LANES] = turned_x

    def rows_early():
        def one(src, carry):
            for c in range(2):
                put_rows(c, 0, src, x_ref[c, row, src])
            t1 = t0_ref[1, row, src]
            put_rows(2, 1, src, jnp.where(low, t1, zero))
            put_rows(3, 1, src, jnp.where(low, zero, t1))
            return carry

        lax.fori_loop(0, n_freq, one, 0, unroll=8)

    def rows_late():
        def one(src, carry):
            t3, t4 = end_ref[0, src], end_ref[1, src]
            put_rows(0, 1, src, jnp.where(low, t3, zero))
            put_rows(1, 1, src, jnp.where(low, zero, t3))
            put_rows(2, 0, src, t4)
            put_rows(3, 0, src, t4)
            return carry

        lax.fori_loop(0, n_freq, one, 0, unroll=8)

    def turn_and_spread(chunk, half):
        turned(chunk, half)
        if chunk == 2:
            spread(half, True, 2, 4)
        elif chunk == 1:
            spread(half, True, 1)
            spread(half, False, 1)
        else:
            spread(half, True, 0)
            for j in range(n_freq // 4):
                src = half * n_freq // 2 + j
                pair = t0_ref[1, row, src], t0_ref[1, row, src + n_freq // 4]
                x4_ref[half * n_freq // 4 + j] = jnp.where(low, *pair)
            spread(half, True, 3)
            spread(half, False, 0, 3)

    def finish(block):
        sort(block)
        keep(0, block).start()

    take = functools.partial(functools.partial, turn_and_spread)
    channelize(0)
    order_gains()
    rearrange(0)
    pl.semaphore_wait(barrier, n_freq + 1)
    turn(0)
    channelize(1, [(1, late, take(0, 0)), (3, late, take(0, 1))])
    pl.when(early)(take(0, 0))
    rearrange(1)
    turn(1)
    pl.when(late)(lambda: forward(0, 0, 3))

    def between():
        forward(1, 0, 3)
        turn_and_spread(1, 0)

    channelize(2, [(2, late, between), (3, late, take(1, 1)), (1, early, take(0, 1)), (2, early, lambda: forward(0, 0, 3))])

    @pl.when(early)
    def _():
        forward(1, 0, 3)
        turn_and_spread(1, 0)

    rearrange(2)
    turn(2)
    pl.when(early)(take(1, 1))
    forward(0, 1)
    turn_and_spread(2, 0)
    spread(0, False, 2, 4)
    forward(1, 1)
    turn_and_spread(2, 1)
    spread(1, False, 2, 4)
    finish(row)
    rows_early()
    rows_late()
    forward(0, 2, 4)
    arrived(0, 1, 3)
    finish(right)
    finish(left)
    forward(1, 2, 4)
    for k in range(1, 5):
        keep(k).start()
    passed(0, 1, 3)
    finish(lax.rem(row + 2, n_pair))
    arrived(2, 4)
    for k in range(5):
        for way in range(2):
            for quarter in range(4):
                side_copy(k, way, quarter).wait_send()
            for half in range(2):
                pass_copy(k, way, half).wait_send()
    for chunk in range(CHUNKS):
        turn_bytes(chunk, 0, n_freq - 1).wait_send()
    for k in range(5):
        for block in range(n_pair if k == 0 else 1):
            keep(k, block).wait()
    passed(2, 4)


def spectra_call(n_freq, n_pair, voltages, taps_table, dft, gains):
    bf16 = jnp.bfloat16
    anywhere = pl.BlockSpec(memory_space=pl.ANY)
    dma = pltpu.SemaphoreType.DMA
    in_hbm = functools.partial(pltpu.with_memory_space_constraint, memory_space=pltpu.HBM)
    return pl.pallas_call(
        functools.partial(spectra_kernel, n_freq, n_pair),
        out_shape=(
            pltpu.VMEM((2, n_pair, n_freq, INPUTS, LANES), bf16),
            pltpu.VMEM((n_pair, n_freq, INPUTS, LANES), bf16),
            pltpu.VMEM((n_pair, n_freq, INPUTS, LANES), bf16),
            pltpu.VMEM((n_pair, n_freq // 2, INPUTS, LANES), bf16),
            pltpu.VMEM((4, 2, n_freq, INPUTS, 2 * LANES), bf16),
        ),
        in_specs=[anywhere] * 4,
        out_specs=(anywhere,) * 5,
        scratch_shapes=[
            pltpu.VMEM((FRAMES, INPUTS, NFFT), jnp.int32),
            pltpu.VMEM((INPUTS, CHANNELS), jnp.float32),
            pltpu.VMEM((TAPS, NFFT), jnp.float32),
            pltpu.VMEM((TAPS, NFFT // LANES, 8, LANES), jnp.float32),
            pltpu.VMEM((NFFT, 2 * LANES), bf16),
            pltpu.VMEM((INPUTS, 2 * LANES), jnp.float32),
            pltpu.VMEM((SPECTRA * INPUTS, 2 * LANES), bf16),
            pltpu.VMEM((SPECTRA * INPUTS, 2 * LANES), bf16),
            pltpu.VMEM((SPECTRA * INPUTS, 2 * LANES), jnp.float32),
            pltpu.VMEM((SPECTRA * INPUTS, LANES), jnp.float32),
            pltpu.VMEM((n_freq, 5, INPUTS, LANES), bf16),
            pltpu.VMEM((2, n_pair, n_freq, INPUTS, LANES), bf16),
            pltpu.VMEM((2, n_pair, n_freq, INPUTS, LANES), bf16),
            pltpu.VMEM((1, n_pair, n_freq, INPUTS, LANES), bf16),
            pltpu.VMEM((2, n_freq, INPUTS, LANES), bf16),
            pltpu.VMEM((n_freq // 2, INPUTS, LANES), bf16),
            pltpu.VMEM((4, 2, n_freq, INPUTS, 2 * LANES), bf16),
            dma((6,)), dma((3,)), dma((CHUNKS,)), dma((CHUNKS, 2)), dma((CHUNKS,)), dma((5, n_pair)),
            dma((5, 2, 4)), dma((5, 2, 4)), dma((5, 2, 2)), dma((5, 2, 2)),
        ],
        compiler_params=pltpu.CompilerParams(
            collective_id=0, has_side_effects=True, vmem_limit_bytes=VMEM_LIMIT
        ),
    )(*map(in_hbm, (voltages, taps_table, dft, gains)))


def correlate_kernel(n_freq, n_pair, x_ref, mid_ref, end_ref, x4_ref, l_ref, out_hbm, out_buf, sem):
    rows, half = n_freq * INPUTS, n_freq * INPUTS // 2

    def copy(c, p):
        cols = pl.ds(pl.multiple_of(p * rows, rows), rows)
        return pltpu.make_async_copy(out_buf.at[c, p], out_hbm.at[c, :, :, cols], sem.at[c, p])

    for c in range(3):

        def block(p, carry):
            for h in range(2):
                quarters = (2 * h, 2 * h + 1) if c < 2 else (h, h + 2)
                spans = [slice(q * n_freq // 4, (q + 1) * n_freq // 4) for q in quarters]
                if c < 2:
                    first, last = ([ref[p, at] for at in spans] for ref in (x_ref.at[c], end_ref))
                    last = jnp.concatenate(last, 0)
                else:
                    first, last = [mid_ref[p, at] for at in spans], x4_ref[p]
                first = jnp.concatenate(first, 0).reshape(half, LANES)
                side = l_ref[3 if c == 2 and h else c].reshape(2 * rows, 2 * LANES)
                sums = lax.dot_general(
                    side, jnp.concatenate([first, last.reshape(half, LANES)], 1), (((1,), (1,)), ((), ())),
                    preferred_element_type=jnp.float32,
                )
                sums = (sums * (1.0 / SAMPLES)).astype(jnp.bfloat16)
                wide = half // 2
                for k, q in enumerate(quarters):
                    part = sums[:, k * wide : (k + 1) * wide]
                    out_buf[c, p, 0, :, q * wide : (q + 1) * wide] = part[:rows]
                    out_buf[c, p, 1, :, q * wide : (q + 1) * wide] = part[rows:]
            copy(c, p).start()
            return carry

        lax.fori_loop(0, n_pair, block, 0, unroll=True)

    for c in range(3):
        for p in range(n_pair):
            copy(c, p).wait()


def correlate_call(n_freq, n_pair, *spectra):
    rows, columns = n_freq * INPUTS, n_pair * n_freq * INPUTS
    vmem = pl.BlockSpec(memory_space=pltpu.VMEM)
    return pl.pallas_call(
        functools.partial(correlate_kernel, n_freq, n_pair),
        out_shape=jax.ShapeDtypeStruct((3, 2, rows, columns), jnp.bfloat16),
        in_specs=[vmem] * 5,
        out_specs=pl.BlockSpec(memory_space=pl.ANY),
        scratch_shapes=[
            pltpu.VMEM((3, n_pair, 2, rows, rows), jnp.bfloat16),
            pltpu.SemaphoreType.DMA((3, n_pair)),
        ],
        compiler_params=pltpu.CompilerParams(vmem_limit_bytes=VMEM_LIMIT),
    )(*(pltpu.with_memory_space_constraint(x, pltpu.VMEM) for x in spectra))


def solution(mesh):
    n_freq, n_pair = mesh.shape["freq"], mesh.shape["pair"]
    taps_table = jnp.asarray(filter_table())
    dft = jnp.asarray(dft_table()).astype(jnp.bfloat16)

    def body(voltages, gains):
        frames = voltages.transpose(1, 0, 2)
        return correlate_call(n_freq, n_pair, *spectra_call(n_freq, n_pair, frames, taps_table, dft, gains))

    placed = (P(("pair", "freq"), None, None), P(("pair", "freq"), None))
    return jax.shard_map(
        body, mesh=mesh, in_specs=placed, out_specs=P("freq", None, "pair", None), check_vma=False
    )
```
